512 devices in a mesh: section: 32 (over y, z_lo), ctx: 16 (over z_hi, x, core).
Axes of the slice: x: 4, y: 8, z: 8 (z_hi: 2, z_lo: 4; z = z_hi * 4 + z_lo), core: 2. Of those that a mesh axis runs over, the one named last changes fastest.
Arguments:
- acts: bfloat16 [32, 2, 2048, 2048], P('section', None, 'ctx'), may hold values from -8 to 8
- out_grad: bfloat16 [32, 2048, 2048], P('section', 'ctx'), may hold values from -6 to 6
- top_grad: bfloat16 [2048, 2048], P('ctx'), may hold values from -6 to 6
- gate_logits: float32 [32, 2, 16, 2048], P('section', None, None, 'ctx'), may hold values from 0 to 12
- q_gain: float32 [32, 2048], P('section'), may hold values from 0.25 to 1.75
- k_gain: float32 [32, 2048], P('section'), may hold values from 0.25 to 1.75
- doc_lengths: int32 [32, 2, 32], P('section'), may hold values from 1 to 128, 2048 in all within a row
Outputs:
- grad_first: bfloat16 [32, 2048, 2048], P('section', 'ctx')
- grad_second: bfloat16 [32, 2048, 2048], P('section', 'ctx')
- gate_grad: float32 [32, 2, 16, 2048], P('section', None, None, 'ctx')
The draws below stay inside these ranges and needn't reach their ends.
Inputs may be any that keep to these rules, and one draw needn't show every extreme that they name: `doc_lengths`: the 32 document lengths of each segment sum to 2048, and the longest is exactly 128.
All inputs are finite; a program needn't handle non-finite values.
Results may differ from the reference program's by a relative error of at most 0.0088.
Values may be sent and summed in bfloat16 or wider, within the bound.
A program may use at most 64 MiB of HBM per device.

```python
import math
import jax
import jax.numpy as jnp
import numpy as np
from jax import lax

HEADS = 16
HEAD_DIM = 128
F = 2048
TOK_DEV = 128
SEGS = 2
MAX_ARTICLE_LEN = 128
SEGMENT_TOKENS = 2048
DOCS = 32
SECTIONS = 32


def draw_acts(key, part):
    key = jax.random.fold_in(key, 3)
    shape = (SECTIONS, SEGS, SEGMENT_TOKENS, F)
    first_key = jax.random.fold_in(key, 0)
    return jnp.clip(jax.random.normal(first_key, shape), -4.0, 4.0).astype(jnp.bfloat16)


def draw_gate_logits(key, part):
    key = jax.random.fold_in(key, 7)
    lookup_array = jax.random.split(key, 7)
    head_shape = (SECTIONS, SEGS, HEADS, 1)
    full_dimensions = (SECTIONS, SEGS, HEADS, SEGMENT_TOKENS)
    share = 0.5
    pick = jax.random.uniform(lookup_array[0], head_shape)
    fast = jax.random.uniform(lookup_array[1], head_shape, minval=1.0 / 50.0, maxval=1.0 / 30.0)
    slow = jax.random.uniform(lookup_array[2], head_shape, minval=0.1, maxval=0.5) / MAX_ARTICLE_LEN
    base = jnp.where(pick < share, fast, slow)
    blocks = SEGMENT_TOKENS // TOK_DEV
    device_factor = jnp.exp(jax.random.uniform(lookup_array[3], (SECTIONS, SEGS, HEADS, blocks, 1), minval=-0.7, maxval=0.7))
    device_factor = jnp.broadcast_to(device_factor, (SECTIONS, SEGS, HEADS, blocks, TOK_DEV)).reshape(full_dimensions)
    token_factor = jnp.exp(jax.random.uniform(lookup_array[4], full_dimensions, minval=-0.5, maxval=0.5))
    fading_speed = base * device_factor * token_factor
    word_cluster = jax.random.uniform(lookup_array[5], full_dimensions)
    forget_weighting = jax.random.uniform(lookup_array[6], full_dimensions, minval=0.22, maxval=0.69)
    fading_speed = jnp.where(word_cluster < 2.0 / MAX_ARTICLE_LEN, forget_weighting, fading_speed)
    return -jnp.log(jnp.expm1(fading_speed))


def level_of(key, extent, shards, smallest, largest):
    level, own = 1.0, jax.random.fold_in(key, 6)
    for position, blocks in shards:
        draws = jnp.exp(jax.random.uniform(jax.random.fold_in(own, position), (blocks,), jnp.float32, smallest / len(shards), largest / len(shards)))
        level = level * jnp.repeat(draws, extent[position] // blocks).reshape([-1 if axis == position else 1 for axis in range(len(extent))])
    return level


def profile(amount, total, reach, slope):
    weights = [(1 << 20) // math.isqrt(standing ** slope) + 1 for standing in range(2, amount + 1)]
    rest, counts = total - reach - (amount - 1), [1] * (amount - 1)
    while rest > 0:
        movable = [i for i in range(amount - 1) if counts[i] < reach]
        pool, left = sum([weights[i] for i in movable]), rest
        for i in movable:
            extra = min(reach - counts[i], max(1, left * weights[i] // pool), rest)
            counts[i] = counts[i] + extra
            rest = rest - extra
    return np.array([reach] + counts)


def uneven_parts(stream_key, amount, total, limit, skew):
    if amount == 2:
        one = jax.random.randint(stream_key, (), max(1, total - limit), min(limit, total - 1) + 1)
        return jnp.stack([one, total - one])
    sizes = jnp.asarray(profile(amount, total, limit, skew), jnp.int32)
    twos = (amount - 1) // 2
    donor, sink = sizes[1:1 + 2 * twos:2], sizes[2:2 + 2 * twos:2]
    room = jnp.minimum(donor - 1, limit - sink)
    shifted = jax.random.randint(jax.random.fold_in(stream_key, 1), (twos,), 0, 1 << 20) % (room + 1)
    sizes = sizes.at[1:1 + 2 * twos:2].set(donor - shifted).at[2:2 + 2 * twos:2].set(sink + shifted)
    return sizes[jax.random.permutation(jax.random.fold_in(stream_key, 2), amount)]


def scatter_about(own_key, extent, spread, bound, cuts=(), held_as=jnp.bfloat16):
    values = jax.random.normal(own_key, extent, jnp.float32) * spread
    if len(cuts) > 0:
        values = level_of(own_key, extent, cuts, -0.22, 0.18) * values
    return jnp.clip(values, min=-bound, max=bound).astype(held_as)


def setup_inputs(seed: int = 0) -> dict:
    keys = jax.random.split(jax.random.key(seed), 8)
    acts = draw_acts(jax.random.fold_in(keys[7], 71), 0)
    out_grad = scatter_about(keys[1], (SECTIONS, SEGMENT_TOKENS, F), 1.0, 6.0, ((0, 32), (1, 16)))
    top_grad = scatter_about(keys[2], (SEGMENT_TOKENS, F), 1.0, 6.0, ((0, 16),))
    gate_logits = draw_gate_logits(jax.random.fold_in(keys[7], 71), 0)
    q_gain = jnp.clip(1.0 + 0.15 * jax.random.normal(keys[4], (SECTIONS, F), jnp.float32), 0.25, 1.75)
    k_gain = jnp.clip(1.0 + 0.15 * jax.random.normal(keys[5], (SECTIONS, F), jnp.float32), 0.25, 1.75)
    doc_lengths = jax.vmap(lambda own: uneven_parts(own, DOCS, SEGMENT_TOKENS, MAX_ARTICLE_LEN, 0))(jax.random.split(keys[6], SECTIONS * SEGS)).reshape((SECTIONS, SEGS, DOCS)).astype(jnp.int32)
    return {"acts": acts, "out_grad": out_grad, "top_grad": top_grad, "gate_logits": gate_logits, "q_gain": q_gain, "k_gain": k_gain, "doc_lengths": doc_lengths}


def doc_index(lengths, positions):
    bounds = jnp.cumsum(lengths)
    return lax.optimization_barrier(jnp.sum((bounds[None, :] <= positions[:, None]).astype(jnp.int32), axis=1)).astype(jnp.int32)

def to_low(values):
    return lax.optimization_barrier(values.astype(jnp.bfloat16)).astype(jnp.float32)

def by_heads(values):
    return values.reshape(values.shape[0], HEADS, HEAD_DIM)

def attend_block(query_x, upstream, query_gate, query_doc, query_pos, key_x, key_gate, key_doc, key_pos, gain_q, gain_k):
    factor = 1.0 / math.sqrt(HEAD_DIM)
    queries = by_heads(to_low(query_x.astype(jnp.float32) * gain_q))
    key_rows = by_heads(to_low(key_x.astype(jnp.float32) * gain_k))
    values = by_heads(key_x.astype(jnp.float32))
    grads_in = by_heads(upstream.astype(jnp.float32))
    allowed = (query_doc[:, None] == key_doc[None, :]) & (key_pos[None, :] <= query_pos[:, None]) & (key_pos[None, :] >= 0)
    scores = jnp.einsum('qhd,khd->hqk', queries, key_rows) * factor
    scores = scores + query_gate[:, :, None] - key_gate[:, None, :]
    scores = jnp.where(allowed[None], scores, -1e+30)
    highest = lax.optimization_barrier(jnp.max(scores, axis=2, keepdims=True))
    log_total = highest + jnp.log(lax.optimization_barrier(jnp.sum(jnp.exp(scores - highest), axis=2, keepdims=True)))
    weights = jnp.where(allowed[None], jnp.exp(scores - log_total), 0.0)
    weights_low = to_low(weights)
    output = jnp.einsum('hqk,khd->qhd', weights_low, values)
    row_dot = jnp.transpose(lax.optimization_barrier(jnp.sum(grads_in * output, axis=2)))
    dweights = jnp.einsum('qhd,khd->hqk', grads_in, values)
    dscores = weights * (dweights - row_dot[:, :, None])
    dscores_low = to_low(dscores)
    dqueries = jnp.einsum('hqk,khd->qhd', dscores_low, key_rows) * factor
    dkeys = jnp.einsum('hqk,qhd->khd', dscores_low, queries) * factor
    dvalues = jnp.einsum('hqk,qhd->khd', weights_low, grads_in)
    row_count = query_x.shape[0]
    key_count = key_x.shape[0]
    return (dqueries.reshape(row_count, -1), lax.optimization_barrier(jnp.sum(dscores, axis=2)), dkeys.reshape(key_count, -1), dvalues.reshape(key_count, -1), lax.optimization_barrier(jnp.sum(dscores, axis=1)))

def fold_keys(stacked):
    own_part = stacked[:, TOK_DEV:]
    near_part = stacked[:, :TOK_DEV]
    filler = jnp.zeros_like(own_part[:1])
    near_part = jnp.concatenate([near_part[1:], filler], axis=0)
    return own_part + near_part

def segment_backward(inputs, upstream, logits, lengths, gain_q, gain_k):
    seg_rows = inputs.shape[0]
    blocks = seg_rows // TOK_DEV
    positions = jnp.arange(seg_rows, dtype=jnp.int32)
    doc_ids = doc_index(lengths, positions)
    log_forget = -jax.nn.softplus(-logits)
    same_doc = doc_ids[:, None] == doc_ids[None, :]
    earlier = (same_doc & (positions[None, :] <= positions[:, None])).astype(log_forget.dtype)
    later = (same_doc & (positions[None, :] >= positions[:, None])).astype(log_forget.dtype)
    gate_sums = jnp.dot(log_forget, earlier.T, precision=lax.Precision.HIGHEST)
    margin = TOK_DEV
    padded_x = jnp.concatenate([jnp.zeros((margin, inputs.shape[1]), inputs.dtype), inputs], axis=0)
    gate_padded = jnp.concatenate([jnp.zeros((HEADS, margin), gate_sums.dtype), gate_sums], axis=1)
    padded_doc = jnp.concatenate([jnp.zeros((margin,), jnp.int32), doc_ids]).astype(jnp.int32)
    padded_pos = jnp.arange(-margin, seg_rows, dtype=jnp.int32)

    def one_block(which_block):
        first_row = (which_block * TOK_DEV).astype(jnp.int32)
        return attend_block(lax.dynamic_slice_in_dim(inputs, first_row, TOK_DEV, 0), lax.dynamic_slice_in_dim(upstream, first_row, TOK_DEV, 0), lax.dynamic_slice_in_dim(gate_sums, first_row, TOK_DEV, 1), lax.dynamic_slice_in_dim(doc_ids, first_row, TOK_DEV, 0), lax.dynamic_slice_in_dim(positions, first_row, TOK_DEV, 0), lax.dynamic_slice_in_dim(padded_x, first_row, 2 * TOK_DEV, 0), lax.dynamic_slice_in_dim(gate_padded, first_row, 2 * TOK_DEV, 1), lax.dynamic_slice_in_dim(padded_doc, first_row, 2 * TOK_DEV, 0), lax.dynamic_slice_in_dim(padded_pos, first_row, 2 * TOK_DEV, 0), gain_q, gain_k)
    dqueries, row_sums, dkeys, dvalues, col_sums = lax.map(one_block, jnp.arange(blocks, dtype=jnp.int32))
    dqueries = dqueries.reshape(seg_rows, -1)
    dkeys = fold_keys(dkeys).reshape(seg_rows, -1)
    dvalues = fold_keys(dvalues).reshape(seg_rows, -1)
    col_total = jnp.transpose(fold_keys(jnp.transpose(col_sums, (0, 2, 1))).reshape(seg_rows, HEADS))
    row_total = jnp.transpose(row_sums, (1, 0, 2)).reshape(HEADS, seg_rows)
    grad_inputs = (upstream.astype(jnp.float32) + gain_q * dqueries + gain_k * dkeys + dvalues).astype(jnp.bfloat16)
    gate_delta = row_total - col_total
    forget_grad = jnp.dot(gate_delta, later.T, precision=lax.Precision.HIGHEST)
    return (grad_inputs, forget_grad * jax.nn.sigmoid(-logits))

def reference(acts, out_grad, top_grad, gate_logits, q_gain, k_gain, doc_lengths):

    def first_section(items):
        return segment_backward(items[0][0], items[1], items[2][0], items[3][0], items[4], items[5])
    grad_first, gate_first = lax.map(first_section, (acts, out_grad, gate_logits, doc_lengths, q_gain, k_gain))
    upstream = jnp.concatenate([grad_first[1:], top_grad[None]], axis=0)

    def second_section(items):
        return segment_backward(items[0][1], items[1], items[2][1], items[3][1], items[4], items[5])
    grad_second, gate_second = lax.map(second_section, (acts, upstream, gate_logits, doc_lengths, q_gain, k_gain))
    return (grad_first, grad_second, jnp.stack([gate_first, gate_second], axis=1))
```

```python
import functools
import math

import jax
import jax.numpy as jnp
from jax import lax
from jax.experimental import pallas as pl
from jax.experimental.pallas import tpu as pltpu
from jax.sharding import PartitionSpec as P

MESH = pl.DeviceIdType.MESH
D = 128
G = 4
W = G * D
B = 1
LOG2E = math.log2(math.e)
F32 = jnp.float32
BF16 = jnp.bfloat16
NT = (((1,), (1,)), ((), ()))
NN = (((1,), (0,)), ((), ()))
TN = (((0,), (0,)), ((), ()))


def dot(a, b, dims):
    return lax.dot_general(a, b, dims, preferred_element_type=F32)


def dot_exact(a, b, dims):
    return lax.dot_general(
        a, b, dims, preferred_element_type=F32, precision=lax.Precision.HIGHEST
    )


def kernel(
    sections,
    shards,
    acts,
    out_grad,
    top_grad,
    logits_in,
    q_gain_in,
    k_gain_in,
    docs_in,
    o_first,
    o_second,
    o_gate,
    ownx,
    logits,
    q_gain,
    k_gain,
    docs,
    prevx,
    dy,
    rrecv,
    rsend,
    outs,
    gate_out,
    passing,
    prevlog,
    crecv,
    csend,
    diff,
    base,
    bias,
    x_s,
    x_r,
    r_s,
    r_r,
    d_s,
    d_r,
    f_s,
    f_r,
    l_s,
    l_r,
    c_s,
    c_r,
    y_s,
    o_s,
    in_s,
    g_s,
):
    s = lax.axis_index("section")
    c = lax.axis_index("ctx")
    rows = acts.shape[2]
    heads = logits.shape[2]
    groups = heads // G
    half_steps = groups // B
    steps = 2 * half_steps
    has_prev = c > 0
    has_next = c < shards - 1
    sends_up = s > 0
    is_last = s == sections - 1
    prev_c = lax.rem(c + shards - 1, shards)
    next_c = lax.rem(c + 1, shards)
    prev_s = lax.rem(s + sections - 1, sections)
    next_s = lax.rem(s + 1, sections)

    relayed = shards == 16 and groups == 4
    half = shards // 2
    core = c % 2
    column = (c % half) // 2
    edge_low = (c == half - 1) if relayed else False
    edge_high = (c == half) if relayed else False
    passes_on = (c < half - 2) if relayed else False
    passes_back = (c > half + 1) if relayed else False
    on_relays = [{"ctx": n} for n in range(half - 2)]
    back_relays = [{"ctx": n} for n in range(half + 2, shards)]

    def when(condition):
        return pl.when(condition) if condition is not False else (lambda f: None)

    fetches = [
        pltpu.make_async_copy(logits_in, logits, in_s.at[0]),
        pltpu.make_async_copy(docs_in, docs, in_s.at[1]),
        pltpu.make_async_copy(q_gain_in, q_gain, in_s.at[2]),
        pltpu.make_async_copy(k_gain_in, k_gain, in_s.at[3]),
        pltpu.make_async_copy(acts.at[0, 0], ownx.at[0], in_s.at[4]),
        pltpu.make_async_copy(acts.at[0, 1], ownx.at[1], in_s.at[5]),
        pltpu.make_async_copy(out_grad.at[0], dy.at[0], in_s.at[6]),
    ]
    for i in (4, 0, 1, 2, 3, 6, 5):
        fetches[i].start()

    barrier = pltpu.get_barrier_semaphore()

    def greet(other):
        pl.semaphore_signal(barrier, inc=1, device_id=other, device_id_type=MESH)

    for other in ({"ctx": prev_c}, {"ctx": next_c}, {"section": prev_s}, {"section": next_s}):
        greet(other)

    @when(edge_low)
    def _():
        for other in back_relays:
            greet(other)

    @when(edge_high)
    def _():
        for other in on_relays:
            greet(other)

    @when(passes_on)
    def _():
        greet({"ctx": half - 1})

    @when(passes_back)
    def _():
        greet({"ctx": half})

    def lanes(n):
        return pl.ds(pl.multiple_of(n * W, W), W)

    def remote(src, dst, send, recv, where):
        return pltpu.make_async_remote_copy(
            src_ref=src,
            dst_ref=dst,
            send_sem=send,
            recv_sem=recv,
            device_id=where,
            device_id_type=MESH,
        )

    t_copy = pltpu.make_async_copy(top_grad, dy.at[1], y_s)

    def each_group(f):
        def go(n, _):
            f(n)
            return 0

        lax.fori_loop(0, groups, go, 0)

    @pl.when(is_last)
    def _():
        t_copy.start()

    peers = jnp.int32(4)
    if relayed:
        peers = peers + jnp.where(edge_low, len(on_relays), 0) + jnp.where(edge_high, len(back_relays), 0)
        peers = peers + jnp.where(passes_on | passes_back, 1, 0)
    pl.semaphore_wait(barrier, peers)

    def x_copy(g, n):
        return remote(
            ownx.at[g, :, lanes(n)],
            prevx.at[g, n],
            x_s.at[g, n],
            x_r.at[g, n],
            {"ctx": next_c},
        )

    def x_far(g, n):
        return remote(
            ownx.at[g, :, lanes(n)], passing, x_s.at[g, n], f_r, {"ctx": 2 * n + g}
        )

    def x_pass():
        return remote(
            passing, prevx.at[core, column], f_s, x_r.at[core, column], {"ctx": half}
        )

    def r_copy(g, n):
        return remote(
            rsend.at[g, n], rrecv.at[g, n], r_s.at[g, n], r_r.at[g, n], {"ctx": prev_c}
        )

    def r_far(g, n):
        return remote(rsend.at[g, n], passing, r_s.at[g, n], f_r, {"ctx": half + 2 * n + g})

    def r_pass():
        return remote(
            passing, rrecv.at[core, column], f_s, r_r.at[core, column], {"ctx": half - 1}
        )

    def d_copy(n):
        return remote(
            outs.at[0, :, lanes(n)],
            dy.at[1, :, lanes(n)],
            d_s.at[n],
            d_r.at[n],
            {"section": prev_s},
        )

    def c_copy(g):
        return remote(csend.at[g], crecv.at[g], c_s.at[g], c_r.at[g], {"ctx": prev_c})

    l_copy = remote(logits.at[0], prevlog, l_s, l_r, {"ctx": next_c})

    def x_pass_in():
        x_far(0, 0).wait_recv()
        x_pass().start()

    def r_pass_in():
        r_far(0, 0).wait_recv()
        r_pass().start()

    def send_acts(g, n):
        far = edge_low & (n < groups - 1) if relayed else False

        @when(far)
        def _():
            x_far(g, n).start()

        @pl.when(has_next & jnp.logical_not(far))
        def _():
            x_copy(g, n).start()

    def send_some(g, begin, stop):
        def go(n, _):
            send_acts(g, n)
            return 0

        lax.fori_loop(begin, stop, go, 0)

    fetches[0].wait()
    fetches[4].wait()

    @pl.when(has_next)
    def _():
        l_copy.start()

    send_some(0, 0, groups // 2)

    @pl.when(jnp.logical_not(has_prev))
    def _():
        prevx[...] = jnp.zeros_like(prevx)
        prevlog[...] = jnp.zeros_like(prevlog)

    @pl.when(jnp.logical_not(has_next))
    def _():
        rrecv[...] = jnp.zeros_like(rrecv)
        crecv[...] = jnp.zeros_like(crecv)

    for i in (1, 2, 3, 6, 5):
        fetches[i].wait()

    def log_forget(x):
        return jnp.minimum(x, 0.0) - jnp.log1p(jnp.exp(-jnp.abs(x)))

    sub = lax.broadcasted_iota(jnp.int32, (rows, rows), 0)
    lane = lax.broadcasted_iota(jnp.int32, (rows, rows), 1)
    anchor = (c * rows).astype(F32)
    own_masks = []
    prev_masks = []
    n_docs = docs.shape[2]
    for g in range(2):
        d0 = lax.broadcasted_iota(jnp.int32, (n_docs, n_docs), 0)
        d1 = lax.broadcasted_iota(jnp.int32, (n_docs, n_docs), 1)
        lengths = docs[0, g : g + 1, :].astype(F32)
        bounds = jnp.sum(jnp.where(d1 <= d0, lengths, 0.0), axis=1, keepdims=True)
        pos = lax.broadcasted_iota(jnp.int32, (n_docs, rows), 1).astype(F32) + anchor
        begin = jnp.max(jnp.where(bounds <= pos, bounds, 0.0), axis=0, keepdims=True)
        key_pos = sub.astype(F32) + anchor
        own_masks.append((key_pos >= begin) & (sub <= lane))
        prev_masks.append(key_pos - float(rows) >= begin)

    @pl.when(has_prev)
    def _():
        l_copy.wait_recv()

    def make_bias(g):
        upto = (lane <= sub).astype(F32)
        after = (lane > sub).astype(F32)
        own = dot_exact(upto, log_forget(logits[0, g]), NT) * LOG2E
        before = dot_exact(after, log_forget(prevlog[g]), NT) * -LOG2E
        for h in range(heads):
            bias[g, h, :rows] = jnp.where(prev_masks[g], -before[:, h : h + 1], -1e30)
            bias[g, h, rows:] = jnp.where(own_masks[g], -own[:, h : h + 1], -1e30)

    make_bias(0)
    send_some(0, groups // 2, groups)

    @when(passes_on & (core == 0) if relayed else False)
    def _():
        x_pass_in()

    make_bias(1)
    factor = 1.0 / math.sqrt(D)

    def load(g, n, j):
        h = n * G + j
        col = pl.ds(pl.multiple_of(h * D, D), D)
        here = slice(j * D, (j + 1) * D)
        x = ownx[g, :, col]
        xp = prevx[g, n, :, here]
        up = dy[g, :, col]
        gq = q_gain[:, col]
        gk = k_gain[:, col]
        xf = x.astype(F32)
        q = (xf * gq).astype(BF16)
        qk = (q.astype(F32) * (gk * factor)).astype(BF16)
        k = jnp.concatenate(
            [(xp.astype(F32) * gk).astype(BF16), (xf * gk).astype(BF16)], axis=0
        )
        v = jnp.concatenate([xp, x], axis=0)
        return h, here, q, qk, k, v, up, gq

    def scores_of(q, k, v, up):
        zero = jnp.zeros((rows, D), BF16)
        right = jnp.concatenate(
            [jnp.concatenate([q, zero], axis=1), jnp.concatenate([zero, up], axis=1)], axis=0
        )
        both = dot(jnp.concatenate([k, v], axis=1), right, NT)
        return both[:, :rows], both[:, rows:]

    def soft(g, h, st, dpt):
        sc = st * (factor * LOG2E) + bias[g, h]
        e = jnp.exp2(sc - jnp.max(sc, axis=0, keepdims=True))
        p = e * (1.0 / jnp.sum(e, axis=0, keepdims=True))
        row_dot = jnp.sum(p * dpt, axis=0, keepdims=True)
        ds = (p * (dpt - row_dot)).astype(BF16)
        sums = jnp.sum(ds.astype(F32), axis=0, keepdims=True)
        return p.astype(BF16), ds, sums

    def compute(step):
        g = step // half_steps
        first = (step % half_steps) * B

        @pl.when(has_prev)
        def _():
            for b in range(B):
                x_copy(g, first + b).wait_recv()

        @pl.when((step == half_steps) & is_last)
        def _():
            t_copy.wait()

        @pl.when((g == 1) & jnp.logical_not(is_last))
        def _():
            for b in range(B):
                d_copy(first + b).wait_recv()

        places = [(first + b, j) for b in range(B) for j in range(G)]
        loaded = [load(g, n, j) for n, j in places]
        raw = [scores_of(q, k, v, up) for _, _, q, _, k, v, up, _ in loaded]
        soft_out = [soft(g, item[0], *both) for item, both in zip(loaded, raw)]
        ones = jnp.ones((16, rows), BF16)
        for (n, _), item, (low, ds, sums) in zip(places, loaded, soft_out):
            h, here, q, qk, k, v, up, gq = item
            t = dot(
                jnp.concatenate([ds, low], axis=1), jnp.concatenate([qk, up], axis=0), NN
            )
            ds_t = ds.T
            dq = dot(ds_t, k, NN)
            cols = dot(ones, ds_t, NN)[:1]
            rsend[g, n, :, here] = t[:rows].astype(BF16)
            base[g, n, :, here] = up.astype(F32) + (gq * factor) * dq + t[rows:]
            csend[g, pl.ds(h, 1), :] = cols[:, :rows]
            diff[g, pl.ds(h, 1), :] = sums - cols[:, rows:]

        for b in range(B):
            n = first + b
            far = edge_high & (n > 0) if relayed else False

            @when(far)
            def _():
                r_far(g, n).start()

            @pl.when(has_prev & jnp.logical_not(far))
            def _():
                r_copy(g, n).start()

        @pl.when(has_prev & (first == groups - B))
        def _():
            c_copy(g).start()

    def finish(step):
        g = step // half_steps
        first = (step % half_steps) * B
        for b in range(B):
            n = first + b

            @pl.when(has_next)
            def _():
                r_copy(g, n).wait_recv()

            total = (base[g, n] + rrecv[g, n].astype(F32)).astype(BF16)
            outs[g, :, lanes(n)] = total

            @pl.when((g == 0) & sends_up)
            def _():
                d_copy(n).start()

            @pl.when(g == 0)
            def _():
                o_copy(0, n).start()

            @pl.when(g == 1)
            def _():
                o_copy(1, n).start()

    def o_copy(g, n):
        to = (o_first, o_second)[g]
        return pltpu.make_async_copy(outs.at[g, :, lanes(n)], to.at[0, :, lanes(n)], o_s.at[g, n])

    lag = 1 + jnp.where(edge_low, 2, 0) if relayed else 1

    def one(step, _):
        compute(step)

        @pl.when((step < half_steps) & jnp.logical_not(edge_low))
        def _():
            for b in range(B):
                send_acts(1, step * B + b)

        @when(edge_low & (step == 0) if relayed else False)
        def _():
            send_some(1, 0, groups)

        @when(passes_on & (core == 1) & (step == 1) if relayed else False)
        def _():
            x_pass_in()

        @when(passes_back & (core == 0) & (step == column + 2) if relayed else False)
        def _():
            r_pass_in()

        @pl.when(step >= lag)
        def _():
            finish(step - lag)

        return 0

    lax.fori_loop(0, steps, one, 0)

    @when(passes_back & (core == 1) if relayed else False)
    def _():
        r_pass_in()

    def gates(g):
        @pl.when(has_next)
        def _():
            c_copy(g).wait_recv()

        mask = own_masks[g].astype(F32)
        strict = jnp.where(sub < lane, mask, 0.0)
        forget = dot_exact(diff[g], mask, NT) + dot_exact(crecv[g], strict, NN)
        gate_out[0, g] = forget * jax.nn.sigmoid(-logits[0, g])

    gates(0)

    def end(step, _):
        finish(step)
        return 0

    lax.fori_loop(steps - lag, steps, end, 0)
    gates(1)
    put_gates = pltpu.make_async_copy(gate_out, o_gate, g_s)
    put_gates.start()

    @pl.when(has_next)
    def _():
        l_copy.wait_send()

        def go(n):
            x_copy(0, n).wait_send()
            x_copy(1, n).wait_send()

        each_group(go)

    @pl.when(has_prev)
    def _():
        c_copy(0).wait_send()
        c_copy(1).wait_send()

        def go(n):
            r_copy(0, n).wait_send()
            r_copy(1, n).wait_send()

        each_group(go)

    @when(passes_on)
    def _():
        x_pass().wait_send()

    @when(passes_back)
    def _():
        r_pass().wait_send()

    @pl.when(sends_up)
    def _():
        each_group(lambda n: d_copy(n).wait_send())

    def put(n):
        o_copy(0, n).wait()
        o_copy(1, n).wait()

    each_group(put)
    put_gates.wait()


def copy_out(a, b, c, out_a, out_b, out_c, held_a, held_b, held_c, got, put):
    moves = []
    for i, (src, held, dst) in enumerate(
        ((a, held_a, out_a), (b, held_b, out_b), (c, held_c, out_c))
    ):
        moves.append(
            (
                pltpu.make_async_copy(src, held, got.at[i]),
                pltpu.make_async_copy(held, dst, put.at[i]),
            )
        )
    for into, _ in moves:
        into.start()
    for into, out in moves:
        into.wait()
        out.start()
    for _, out in moves:
        out.wait()


def body(sections, shards, acts, out_grad, top_grad, logits, q_gain, k_gain, docs):
    rows = acts.shape[2]
    heads = logits.shape[2]
    groups = heads // G
    anywhere = pl.BlockSpec(memory_space=pl.ANY)
    sem = pltpu.SemaphoreType.DMA
    vmem = pltpu.VMEM
    shapes = (
        jax.ShapeDtypeStruct(out_grad.shape, BF16),
        jax.ShapeDtypeStruct(out_grad.shape, BF16),
        jax.ShapeDtypeStruct(logits.shape, F32),
    )
    results = pl.pallas_call(
        functools.partial(kernel, sections, shards),
        out_shape=shapes,
        in_specs=[anywhere] * 7,
        out_specs=(anywhere,) * 3,
        scratch_shapes=[
            vmem(acts.shape[1:], BF16),
            vmem(logits.shape, F32),
            vmem(q_gain.shape, F32),
            vmem(k_gain.shape, F32),
            vmem(docs.shape, jnp.int32),
            vmem((2, groups, rows, W), BF16),
            vmem(acts.shape[1:], BF16),
            vmem((2, groups, rows, W), BF16),
            vmem((2, groups, rows, W), BF16),
            vmem(acts.shape[1:], BF16),
            vmem(logits.shape, F32),
            vmem((rows, W), BF16),
            vmem((2, heads, rows), F32),
            vmem((2, heads, rows), F32),
            vmem((2, heads, rows), F32),
            vmem((2, heads, rows), F32),
            vmem((2, groups, rows, W), F32),
            vmem((2, heads, 2 * rows, rows), F32),
            sem((2, groups)),
            sem((2, groups)),
            sem((2, groups)),
            sem((2, groups)),
            sem((groups,)),
            sem((groups,)),
            sem,
            sem,
            sem,
            sem,
            sem((2,)),
            sem((2,)),
            sem,
            sem((2, groups)),
            sem((7,)),
            sem,
        ],
        compiler_params=pltpu.CompilerParams(
            collective_id=0, has_side_effects=True, vmem_limit_bytes=60 * 1024 * 1024
        ),
    )(acts, out_grad, top_grad, logits, q_gain, k_gain, docs)
    return pl.pallas_call(
        copy_out,
        out_shape=shapes,
        in_specs=[anywhere] * 3,
        out_specs=(anywhere,) * 3,
        scratch_shapes=[vmem(shape.shape, shape.dtype) for shape in shapes]
        + [sem((3,)), sem((3,))],
        compiler_params=pltpu.CompilerParams(vmem_limit_bytes=60 * 1024 * 1024),
    )(*results)


def solution(mesh):
    in_specs = (
        P("section", None, "ctx", None),
        P("section", "ctx", None),
        P("ctx", None),
        P("section", None, None, "ctx"),
        P("section", None),
        P("section", None),
        P("section", None, None),
    )
    out_specs = (
        P("section", "ctx", None),
        P("section", "ctx", None),
        P("section", None, None, "ctx"),
    )
    return jax.shard_map(
        functools.partial(body, mesh.shape["section"], mesh.shape["ctx"]),
        mesh=mesh,
        in_specs=in_specs,
        out_specs=out_specs,
        check_vma=False,
    )
```

```python
import functools
import math

import jax
import jax.numpy as jnp
from jax import lax
from jax.experimental import pallas as pl
from jax.experimental.pallas import tpu as pltpu
from jax.sharding import PartitionSpec as P

MESH = pl.DeviceIdType.MESH
D = 128
G = 4
W = G * D
B = 1
LOG2E = math.log2(math.e)
F32 = jnp.float32
BF16 = jnp.bfloat16
NT = (((1,), (1,)), ((), ()))
NN = (((1,), (0,)), ((), ()))
TN = (((0,), (0,)), ((), ()))


def dot(a, b, dims):
    return lax.dot_general(a, b, dims, preferred_element_type=F32)


def dot_exact(a, b, dims):
    return lax.dot_general(
        a, b, dims, preferred_element_type=F32, precision=lax.Precision.HIGHEST
    )


def kernel(
    sections,
    shards,
    acts,
    out_grad,
    top_grad,
    logits_in,
    q_gain_in,
    k_gain_in,
    docs_in,
    o_first,
    o_second,
    o_gate,
    ownx,
    logits,
    q_gain,
    k_gain,
    docs,
    prevx,
    dy,
    rrecv,
    rsend,
    outs,
    gate_out,
    passing,
    prevlog,
    crecv,
    csend,
    diff,
    base,
    bias,
    x_s,
    x_r,
    r_s,
    r_r,
    d_s,
    d_r,
    f_s,
    f_r,
    l_s,
    l_r,
    c_s,
    c_r,
    y_s,
    o_s,
    in_s,
    g_s,
):
    s = lax.axis_index("section")
    c = lax.axis_index("ctx")
    rows = acts.shape[2]
    heads = logits.shape[2]
    groups = heads // G
    half_steps = groups // B
    steps = 2 * half_steps
    has_prev = c > 0
    has_next = c < shards - 1
    sends_up = s > 0
    is_last = s == sections - 1
    prev_c = lax.rem(c + shards - 1, shards)
    next_c = lax.rem(c + 1, shards)
    prev_s = lax.rem(s + sections - 1, sections)
    next_s = lax.rem(s + 1, sections)

    relayed = shards == 16 and groups == 4
    half = shards // 2
    core = c % 2
    column = (c % half) // 2
    edge_low = (c == half - 1) if relayed else False
    edge_high = (c == half) if relayed else False
    passes_on = (c < half - 2) if relayed else False
    passes_back = (c > half + 1) if relayed else False
    on_relays = [{"ctx": n} for n in range(half - 2)]
    back_relays = [{"ctx": n} for n in range(half + 2, shards)]

    def when(condition):
        return pl.when(condition) if condition is not False else (lambda f: None)

    fetches = [
        pltpu.make_async_copy(logits_in, logits, in_s.at[0]),
        pltpu.make_async_copy(docs_in, docs, in_s.at[1]),
        pltpu.make_async_copy(q_gain_in, q_gain, in_s.at[2]),
        pltpu.make_async_copy(k_gain_in, k_gain, in_s.at[3]),
        pltpu.make_async_copy(acts.at[0, 0], ownx.at[0], in_s.at[4]),
        pltpu.make_async_copy(acts.at[0, 1], ownx.at[1], in_s.at[5]),
        pltpu.make_async_copy(out_grad.at[0], dy.at[0], in_s.at[6]),
    ]
    for i in (4, 0, 1, 2, 3, 6, 5):
        fetches[i].start()

    barrier = pltpu.get_barrier_semaphore()

    def greet(other):
        pl.semaphore_signal(barrier, inc=1, device_id=other, device_id_type=MESH)

    for other in ({"ctx": prev_c}, {"ctx": next_c}, {"section": prev_s}, {"section": next_s}):
        greet(other)

    @when(edge_low)
    def _():
        for other in back_relays:
            greet(other)

    @when(edge_high)
    def _():
        for other in on_relays:
            greet(other)

    @when(passes_on)
    def _():
        greet({"ctx": half - 1})

    @when(passes_back)
    def _():
        greet({"ctx": half})

    def lanes(n):
        return pl.ds(pl.multiple_of(n * W, W), W)

    def remote(src, dst, send, recv, where):
        return pltpu.make_async_remote_copy(
            src_ref=src,
            dst_ref=dst,
            send_sem=send,
            recv_sem=recv,
            device_id=where,
            device_id_type=MESH,
        )

    t_copy = pltpu.make_async_copy(top_grad, dy.at[1], y_s)

    def each_group(f):
        def go(n, _):
            f(n)
            return 0

        lax.fori_loop(0, groups, go, 0)

    @pl.when(is_last)
    def _():
        t_copy.start()

    peers = jnp.int32(4)
    if relayed:
        peers = peers + jnp.where(edge_low, len(on_relays), 0) + jnp.where(edge_high, len(back_relays), 0)
        peers = peers + jnp.where(passes_on | passes_back, 1, 0)
    pl.semaphore_wait(barrier, peers)

    def x_copy(g, n):
        return remote(
            ownx.at[g, :, lanes(n)],
            prevx.at[g, n],
            x_s.at[g, n],
            x_r.at[g, n],
            {"ctx": next_c},
        )

    def x_far(g, n):
        return remote(
            ownx.at[g, :, lanes(n)], passing, x_s.at[g, n], f_r, {"ctx": 2 * n + g}
        )

    def x_pass():
        return remote(
            passing, prevx.at[core, column], f_s, x_r.at[core, column], {"ctx": half}
        )

    def r_copy(g, n):
        return remote(
            rsend.at[g, n], rrecv.at[g, n], r_s.at[g, n], r_r.at[g, n], {"ctx": prev_c}
        )

    def r_far(g, n):
        return remote(rsend.at[g, n], passing, r_s.at[g, n], f_r, {"ctx": half + 2 * n + g})

    def r_pass():
        return remote(
            passing, rrecv.at[core, column], f_s, r_r.at[core, column], {"ctx": half - 1}
        )

    def d_copy(n):
        return remote(
            outs.at[0, :, lanes(n)],
            dy.at[1, :, lanes(n)],
            d_s.at[n],
            d_r.at[n],
            {"section": prev_s},
        )

    def c_copy(g):
        return remote(csend.at[g], crecv.at[g], c_s.at[g], c_r.at[g], {"ctx": prev_c})

    l_copy = remote(logits.at[0], prevlog, l_s, l_r, {"ctx": next_c})

    def x_pass_in():
        x_far(0, 0).wait_recv()
        x_pass().start()

    def r_pass_in():
        r_far(0, 0).wait_recv()
        r_pass().start()

    def send_acts(g, n):
        far = edge_low & (n < groups - 1) if relayed else False

        @when(far)
        def _():
            x_far(g, n).start()

        @pl.when(has_next & jnp.logical_not(far))
        def _():
            x_copy(g, n).start()

    def send_some(g, begin, stop):
        def go(n, _):
            send_acts(g, n)
            return 0

        lax.fori_loop(begin, stop, go, 0)

    fetches[0].wait()
    fetches[4].wait()

    @pl.when(has_next)
    def _():
        l_copy.start()

    send_some(0, 0, groups // 2)

    @pl.when(jnp.logical_not(has_prev))
    def _():
        prevx[...] = jnp.zeros_like(prevx)
        prevlog[...] = jnp.zeros_like(prevlog)

    @pl.when(jnp.logical_not(has_next))
    def _():
        rrecv[...] = jnp.zeros_like(rrecv)
        crecv[...] = jnp.zeros_like(crecv)

    for i in (1, 2, 3, 6, 5):
        fetches[i].wait()

    def log_forget(x):
        return jnp.minimum(x, 0.0) - jnp.log1p(jnp.exp(-jnp.abs(x)))

    sub = lax.broadcasted_iota(jnp.int32, (rows, rows), 0)
    lane = lax.broadcasted_iota(jnp.int32, (rows, rows), 1)
    anchor = (c * rows).astype(F32)
    own_masks = []
    prev_masks = []
    n_docs = docs.shape[2]
    for g in range(2):
        d0 = lax.broadcasted_iota(jnp.int32, (n_docs, n_docs), 0)
        d1 = lax.broadcasted_iota(jnp.int32, (n_docs, n_docs), 1)
        lengths = docs[0, g : g + 1, :].astype(F32)
        bounds = jnp.sum(jnp.where(d1 <= d0, lengths, 0.0), axis=1, keepdims=True)
        pos = lax.broadcasted_iota(jnp.int32, (n_docs, rows), 1).astype(F32) + anchor
        begin = jnp.max(jnp.where(bounds <= pos, bounds, 0.0), axis=0, keepdims=True)
        key_pos = sub.astype(F32) + anchor
        own_masks.append((key_pos >= begin) & (sub <= lane))
        prev_masks.append((key_pos - float(rows) >= begin) & (sub > lane))

    @pl.when(has_prev)
    def _():
        l_copy.wait_recv()

    def make_bias(g):
        upto = (lane <= sub).astype(F32)
        after = (lane > sub).astype(F32)
        own = dot_exact(upto, log_forget(logits[0, g]), NT) * LOG2E
        before = dot_exact(after, log_forget(prevlog[g]), NT) * -LOG2E
        for h in range(heads):
            bias[g, h] = jnp.where(
                own_masks[g],
                -own[:, h : h + 1],
                jnp.where(prev_masks[g], -before[:, h : h + 1], -1e30),
            )

    make_bias(0)
    send_some(0, groups // 2, groups)

    @when(passes_on & (core == 0) if relayed else False)
    def _():
        x_pass_in()

    make_bias(1)
    factor = 1.0 / math.sqrt(D)
    upto = sub <= lane
    own_part = upto.astype(F32).astype(BF16)
    prev_part = (sub > lane).astype(F32).astype(BF16)
    own_part_t = (lane <= sub).astype(F32).astype(BF16)
    prev_part_t = (lane > sub).astype(F32).astype(BF16)

    def head(g, n, h):
        col = pl.ds(pl.multiple_of(h * D, D), D)
        here = pl.ds(pl.multiple_of((h - n * G) * D, D), D)
        x = ownx[g, :, col]
        xp = prevx[g, n, :, here]
        up = dy[g, :, col]
        gq = q_gain[:, col]
        gk = k_gain[:, col]
        xf = x.astype(F32)
        q = (xf * gq).astype(BF16)
        k = jnp.concatenate(
            [(xp.astype(F32) * gk).astype(BF16), (xf * gk).astype(BF16)], axis=0
        )
        v = jnp.concatenate([xp, x], axis=0)
        st = dot(k, q, NT)
        dpt = dot(v, up, NT)
        st = jnp.where(upto, st[rows:], st[:rows])
        dpt = jnp.where(upto, dpt[rows:], dpt[:rows])
        sc = st * (factor * LOG2E) + bias[g, h]
        e = jnp.exp2(sc - jnp.max(sc, axis=0, keepdims=True))
        p = e * (1.0 / jnp.sum(e, axis=0, keepdims=True))
        row_dot = jnp.sum(p * dpt, axis=0, keepdims=True)
        ds = (p * (dpt - row_dot)).astype(BF16)
        low = p.astype(BF16)
        sums = jnp.sum(ds.astype(F32), axis=0, keepdims=True)
        turned = ds.T
        ds_t = jnp.concatenate([turned * prev_part_t, turned * own_part_t], axis=1)
        dk = dot(jnp.concatenate([ds * prev_part, ds * own_part], axis=0), q, NN)
        dv = dot(jnp.concatenate([low * prev_part, low * own_part], axis=0), up, NN)
        dq = dot(ds_t, k, NN)
        cols = dot(jnp.ones((16, rows), BF16), ds_t, NN)[:1]
        t = (gk * factor) * dk + dv
        rsend[g, n, :, here] = t[:rows].astype(BF16)
        base[g, n, :, here] = up.astype(F32) + (gq * factor) * dq + t[rows:]
        csend[g, pl.ds(h, 1), :] = cols[:, :rows]
        diff[g, pl.ds(h, 1), :] = sums - cols[:, rows:]

    def compute(step):
        g = step // half_steps
        first = (step % half_steps) * B

        @pl.when(has_prev)
        def _():
            for b in range(B):
                x_copy(g, first + b).wait_recv()

        @pl.when((step == half_steps) & is_last)
        def _():
            t_copy.wait()

        @pl.when((g == 1) & jnp.logical_not(is_last))
        def _():
            for b in range(B):
                d_copy(first + b).wait_recv()

        def pair(i, _):
            h = first * G + 2 * i
            head(g, first, h)
            head(g, first, h + 1)
            return 0

        lax.fori_loop(0, G // 2, pair, 0)

        for b in range(B):
            n = first + b
            far = edge_high & (n > 0) if relayed else False

            @when(far)
            def _():
                r_far(g, n).start()

            @pl.when(has_prev & jnp.logical_not(far))
            def _():
                r_copy(g, n).start()

        @pl.when(has_prev & (first == groups - B))
        def _():
            c_copy(g).start()

    def finish(step):
        g = step // half_steps
        first = (step % half_steps) * B
        for b in range(B):
            n = first + b

            @pl.when(has_next)
            def _():
                r_copy(g, n).wait_recv()

            total = (base[g, n] + rrecv[g, n].astype(F32)).astype(BF16)
            outs[g, :, lanes(n)] = total

            @pl.when((g == 0) & sends_up)
            def _():
                d_copy(n).start()

            @pl.when(g == 0)
            def _():
                o_copy(0, n).start()

            @pl.when(g == 1)
            def _():
                o_copy(1, n).start()

    def o_copy(g, n):
        to = (o_first, o_second)[g]
        return pltpu.make_async_copy(outs.at[g, :, lanes(n)], to.at[0, :, lanes(n)], o_s.at[g, n])

    lag = 1

    def end(step, _):
        finish(step)
        return 0

    def one(step, _):
        compute(step)

        @pl.when((step < half_steps) & jnp.logical_not(edge_low))
        def _():
            for b in range(B):
                send_acts(1, step * B + b)

        @when(edge_low & (step == 0) if relayed else False)
        def _():
            send_some(1, 0, groups)

        @when(passes_on & (core == 1) & (step == 1) if relayed else False)
        def _():
            x_pass_in()

        @when(passes_back & (core == 0) & (step == column + 2) if relayed else False)
        def _():
            r_pass_in()

        @pl.when((step >= lag) & jnp.logical_not(edge_low & (step <= half_steps)))
        def _():
            finish(step - lag)

        @when(edge_low & (step == half_steps - 1) if relayed else False)
        def _():
            lax.fori_loop(0, half_steps, end, 0)

        return 0

    lax.fori_loop(0, steps, one, 0)

    @when(passes_back & (core == 1) if relayed else False)
    def _():
        r_pass_in()

    def gates(g):
        @pl.when(has_next)
        def _():
            c_copy(g).wait_recv()

        mask = own_masks[g].astype(F32)
        strict = jnp.where(sub < lane, mask, 0.0)
        forget = dot_exact(diff[g], mask, NT) + dot_exact(crecv[g], strict, NN)
        gate_out[0, g] = forget * jax.nn.sigmoid(-logits[0, g])

    gates(0)

    lax.fori_loop(steps - lag, steps, end, 0)
    gates(1)
    put_gates = pltpu.make_async_copy(gate_out, o_gate, g_s)
    put_gates.start()

    @pl.when(has_next)
    def _():
        l_copy.wait_send()

        def go(n):
            x_copy(0, n).wait_send()
            x_copy(1, n).wait_send()

        each_group(go)

    @pl.when(has_prev)
    def _():
        c_copy(0).wait_send()
        c_copy(1).wait_send()

        def go(n):
            r_copy(0, n).wait_send()
            r_copy(1, n).wait_send()

        each_group(go)

    @when(passes_on)
    def _():
        x_pass().wait_send()

    @when(passes_back)
    def _():
        r_pass().wait_send()

    @pl.when(sends_up)
    def _():
        each_group(lambda n: d_copy(n).wait_send())

    def put(n):
        o_copy(0, n).wait()
        o_copy(1, n).wait()

    each_group(put)
    put_gates.wait()


def copy_out(a, b, c, out_a, out_b, out_c, held_a, held_b, held_c, got, put):
    moves = []
    for i, (src, held, dst) in enumerate(
        ((a, held_a, out_a), (b, held_b, out_b), (c, held_c, out_c))
    ):
        moves.append(
            (
                pltpu.make_async_copy(src, held, got.at[i]),
                pltpu.make_async_copy(held, dst, put.at[i]),
            )
        )
    for into, _ in moves:
        into.start()
    for into, out in moves:
        into.wait()
        out.start()
    for _, out in moves:
        out.wait()


def body(sections, shards, acts, out_grad, top_grad, logits, q_gain, k_gain, docs):
    rows = acts.shape[2]
    heads = logits.shape[2]
    groups = heads // G
    anywhere = pl.BlockSpec(memory_space=pl.ANY)
    sem = pltpu.SemaphoreType.DMA
    vmem = pltpu.VMEM
    shapes = (
        jax.ShapeDtypeStruct(out_grad.shape, BF16),
        jax.ShapeDtypeStruct(out_grad.shape, BF16),
        jax.ShapeDtypeStruct(logits.shape, F32),
    )
    results = pl.pallas_call(
        functools.partial(kernel, sections, shards),
        out_shape=shapes,
        in_specs=[anywhere] * 7,
        out_specs=(anywhere,) * 3,
        scratch_shapes=[
            vmem(acts.shape[1:], BF16),
            vmem(logits.shape, F32),
            vmem(q_gain.shape, F32),
            vmem(k_gain.shape, F32),
            vmem(docs.shape, jnp.int32),
            vmem((2, groups, rows, W), BF16),
            vmem(acts.shape[1:], BF16),
            vmem((2, groups, rows, W), BF16),
            vmem((2, groups, rows, W), BF16),
            vmem(acts.shape[1:], BF16),
            vmem(logits.shape, F32),
            vmem((rows, W), BF16),
            vmem((2, heads, rows), F32),
            vmem((2, heads, rows), F32),
            vmem((2, heads, rows), F32),
            vmem((2, heads, rows), F32),
            vmem((2, groups, rows, W), F32),
            vmem((2, heads, rows, rows), F32),
            sem((2, groups)),
            sem((2, groups)),
            sem((2, groups)),
            sem((2, groups)),
            sem((groups,)),
            sem((groups,)),
            sem,
            sem,
            sem,
            sem,
            sem((2,)),
            sem((2,)),
            sem,
            sem((2, groups)),
            sem((7,)),
            sem,
        ],
        compiler_params=pltpu.CompilerParams(
            collective_id=0, has_side_effects=True, vmem_limit_bytes=60 * 1024 * 1024
        ),
    )(acts, out_grad, top_grad, logits, q_gain, k_gain, docs)
    return pl.pallas_call(
        copy_out,
        out_shape=shapes,
        in_specs=[anywhere] * 3,
        out_specs=(anywhere,) * 3,
        scratch_shapes=[vmem(shape.shape, shape.dtype) for shape in shapes]
        + [sem((3,)), sem((3,))],
        compiler_params=pltpu.CompilerParams(vmem_limit_bytes=60 * 1024 * 1024),
    )(*results)


def solution(mesh):
    in_specs = (
        P("section", None, "ctx", None),
        P("section", "ctx", None),
        P("ctx", None),
        P("section", None, None, "ctx"),
        P("section", None),
        P("section", None),
        P("section", None, None),
    )
    out_specs = (
        P("section", "ctx", None),
        P("section", "ctx", None),
        P("section", None, None, "ctx"),
    )
    return jax.shard_map(
        functools.partial(body, mesh.shape["section"], mesh.shape["ctx"]),
        mesh=mesh,
        in_specs=in_specs,
        out_specs=out_specs,
        check_vma=False,
    )
```

```python
import functools
import math

import jax
import jax.numpy as jnp
from jax import lax
from jax.experimental import pallas as pl
from jax.experimental.pallas import tpu as pltpu
from jax.sharding import PartitionSpec as P

MESH = pl.DeviceIdType.MESH
D = 128
G = 4
W = G * D
B = 1
LOG2E = math.log2(math.e)
F32 = jnp.float32
BF16 = jnp.bfloat16
NT = (((1,), (1,)), ((), ()))
NN = (((1,), (0,)), ((), ()))
TN = (((0,), (0,)), ((), ()))


def dot(a, b, dims):
    return lax.dot_general(a, b, dims, preferred_element_type=F32)


def dot_exact(a, b, dims):
    return lax.dot_general(
        a, b, dims, preferred_element_type=F32, precision=lax.Precision.HIGHEST
    )


def kernel(
    sections,
    shards,
    acts,
    out_grad,
    top_grad,
    logits_in,
    q_gain_in,
    k_gain_in,
    docs_in,
    o_first,
    o_second,
    o_gate,
    ownx,
    logits,
    q_gain,
    k_gain,
    docs,
    prevx,
    dy,
    rrecv,
    rsend,
    outs,
    gate_out,
    passing,
    prevlog,
    crecv,
    csend,
    diff,
    base,
    bias,
    x_s,
    x_r,
    r_s,
    r_r,
    d_s,
    d_r,
    f_s,
    f_r,
    l_s,
    l_r,
    c_s,
    c_r,
    y_s,
    o_s,
    in_s,
    g_s,
):
    s = lax.axis_index("section")
    c = lax.axis_index("ctx")
    rows = acts.shape[2]
    heads = logits.shape[2]
    groups = heads // G
    half_steps = groups // B
    steps = 2 * half_steps
    has_prev = c > 0
    has_next = c < shards - 1
    sends_up = s > 0
    is_last = s == sections - 1
    prev_c = lax.rem(c + shards - 1, shards)
    next_c = lax.rem(c + 1, shards)
    prev_s = lax.rem(s + sections - 1, sections)
    next_s = lax.rem(s + 1, sections)

    relayed = shards == 16 and groups == 4
    half = shards // 2
    core = c % 2
    column = (c % half) // 2
    back = jnp.maximum(column - 1, 0)
    edge_low = (c == half - 1) if relayed else False
    edge_high = (c == half) if relayed else False
    passes_on = (c < half - 2) if relayed else False
    passes_back = (c > half + 1) if relayed else False
    on_relays = [{"ctx": n} for n in range(half - 2)]
    back_relays = [{"ctx": n} for n in range(half + 2, shards)]

    def when(condition):
        return pl.when(condition) if condition is not False else (lambda f: None)

    fetches = [
        pltpu.make_async_copy(logits_in, logits, in_s.at[0]),
        pltpu.make_async_copy(docs_in, docs, in_s.at[1]),
        pltpu.make_async_copy(q_gain_in, q_gain, in_s.at[2]),
        pltpu.make_async_copy(k_gain_in, k_gain, in_s.at[3]),
        pltpu.make_async_copy(acts.at[0, 0], ownx.at[0], in_s.at[4]),
        pltpu.make_async_copy(acts.at[0, 1], ownx.at[1], in_s.at[5]),
        pltpu.make_async_copy(out_grad.at[0], dy.at[0], in_s.at[6]),
    ]
    for i in (4, 0, 1, 2, 3, 6, 5):
        fetches[i].start()

    barrier = pltpu.get_barrier_semaphore()

    def greet(other):
        pl.semaphore_signal(barrier, inc=1, device_id=other, device_id_type=MESH)

    for other in ({"ctx": prev_c}, {"ctx": next_c}, {"section": prev_s}, {"section": next_s}):
        greet(other)

    @when(edge_low)
    def _():
        for other in back_relays:
            greet(other)

    @when(edge_high)
    def _():
        for other in on_relays:
            greet(other)

    @when(passes_on)
    def _():
        greet({"ctx": half - 1})

    @when(passes_back)
    def _():
        greet({"ctx": half})

    def lanes(n):
        return pl.ds(pl.multiple_of(n * W, W), W)

    def remote(src, dst, send, recv, where):
        return pltpu.make_async_remote_copy(
            src_ref=src,
            dst_ref=dst,
            send_sem=send,
            recv_sem=recv,
            device_id=where,
            device_id_type=MESH,
        )

    t_copy = pltpu.make_async_copy(top_grad, dy.at[1], y_s)

    def each_group(f):
        def go(n, _):
            f(n)
            return 0

        lax.fori_loop(0, groups, go, 0)

    @pl.when(is_last)
    def _():
        t_copy.start()

    peers = jnp.int32(4)
    if relayed:
        peers = peers + jnp.where(edge_low, len(on_relays), 0) + jnp.where(edge_high, len(back_relays), 0)
        peers = peers + jnp.where(passes_on | passes_back, 1, 0)
    pl.semaphore_wait(barrier, peers)

    def x_copy(g, n):
        return remote(
            ownx.at[g, :, lanes(n)],
            prevx.at[g, n],
            x_s.at[g, n],
            x_r.at[g, n],
            {"ctx": next_c},
        )

    def x_far(g, n):
        return remote(
            ownx.at[g, :, lanes(n)], passing, x_s.at[g, n], f_r, {"ctx": 2 * n + g}
        )

    def x_pass():
        return remote(
            passing, prevx.at[core, column], f_s, x_r.at[core, column], {"ctx": half}
        )

    def r_copy(g, n):
        return remote(
            rsend.at[g, n], rrecv.at[g, n], r_s.at[g, n], r_r.at[g, n], {"ctx": prev_c}
        )

    def r_far(g, n):
        return remote(rsend.at[g, n], passing, r_s.at[g, n], f_r, {"ctx": half + 2 * n + 2 + g})

    def r_pass():
        return remote(
            passing, rrecv.at[core, back], f_s, r_r.at[core, back], {"ctx": half - 1}
        )

    def d_copy(n):
        return remote(
            outs.at[0, :, lanes(n)],
            dy.at[1, :, lanes(n)],
            d_s.at[n],
            d_r.at[n],
            {"section": prev_s},
        )

    def c_copy(g):
        return remote(csend.at[g], crecv.at[g], c_s.at[g], c_r.at[g], {"ctx": prev_c})

    l_copy = remote(logits.at[0], prevlog, l_s, l_r, {"ctx": next_c})

    def x_pass_in():
        x_far(0, 0).wait_recv()
        x_pass().start()

    def r_pass_in():
        r_far(0, 0).wait_recv()
        r_pass().start()

    def send_acts(g, n):
        far = edge_low & (n < groups - 1) if relayed else False

        @when(far)
        def _():
            x_far(g, n).start()

        @pl.when(has_next & jnp.logical_not(far))
        def _():
            x_copy(g, n).start()

    def send_some(g, begin, stop):
        def go(n, _):
            send_acts(g, n)
            return 0

        lax.fori_loop(begin, stop, go, 0)

    fetches[0].wait()
    fetches[4].wait()

    @pl.when(has_next)
    def _():
        l_copy.start()

    send_some(0, 0, groups // 2)

    @pl.when(jnp.logical_not(has_prev))
    def _():
        prevx[...] = jnp.zeros_like(prevx)
        prevlog[...] = jnp.zeros_like(prevlog)

    @pl.when(jnp.logical_not(has_next))
    def _():
        rrecv[...] = jnp.zeros_like(rrecv)
        crecv[...] = jnp.zeros_like(crecv)

    for i in (1, 2, 3, 6, 5):
        fetches[i].wait()

    def log_forget(x):
        return jnp.minimum(x, 0.0) - jnp.log1p(jnp.exp(-jnp.abs(x)))

    sub = lax.broadcasted_iota(jnp.int32, (rows, rows), 0)
    lane = lax.broadcasted_iota(jnp.int32, (rows, rows), 1)
    anchor = (c * rows).astype(F32)
    own_masks = []
    prev_masks = []
    n_docs = docs.shape[2]
    for g in range(2):
        d0 = lax.broadcasted_iota(jnp.int32, (n_docs, n_docs), 0)
        d1 = lax.broadcasted_iota(jnp.int32, (n_docs, n_docs), 1)
        lengths = docs[0, g : g + 1, :].astype(F32)
        bounds = jnp.sum(jnp.where(d1 <= d0, lengths, 0.0), axis=1, keepdims=True)
        pos = lax.broadcasted_iota(jnp.int32, (n_docs, rows), 1).astype(F32) + anchor
        begin = jnp.max(jnp.where(bounds <= pos, bounds, 0.0), axis=0, keepdims=True)
        key_pos = sub.astype(F32) + anchor
        own_masks.append((key_pos >= begin) & (sub <= lane))
        prev_masks.append((key_pos - float(rows) >= begin) & (sub > lane))

    @pl.when(has_prev)
    def _():
        l_copy.wait_recv()

    def make_bias(g):
        upto = (lane <= sub).astype(F32)
        after = (lane > sub).astype(F32)
        own = dot_exact(upto, log_forget(logits[0, g]), NT) * LOG2E
        before = dot_exact(after, log_forget(prevlog[g]), NT) * -LOG2E
        for h in range(heads):
            bias[g, h] = jnp.where(
                own_masks[g],
                -own[:, h : h + 1],
                jnp.where(prev_masks[g], -before[:, h : h + 1], -1e30),
            )

    make_bias(0)
    send_some(0, groups // 2, groups)

    @when(passes_on & (core == 0) if relayed else False)
    def _():
        x_pass_in()

    make_bias(1)
    factor = 1.0 / math.sqrt(D)
    upto = sub <= lane
    own_part = upto.astype(F32).astype(BF16)
    prev_part = (sub > lane).astype(F32).astype(BF16)
    own_part_t = (lane <= sub).astype(F32).astype(BF16)
    prev_part_t = (lane > sub).astype(F32).astype(BF16)

    def load(g, n, j):
        h = n * G + j
        col = pl.ds(pl.multiple_of(h * D, D), D)
        here = slice(j * D, (j + 1) * D)
        x = ownx[g, :, col]
        xp = prevx[g, n, :, here]
        up = dy[g, :, col]
        gq = q_gain[:, col]
        gk = k_gain[:, col]
        xf = x.astype(F32)
        q = (xf * gq).astype(BF16)
        qk = (q.astype(F32) * (gk * factor)).astype(BF16)
        k = jnp.concatenate(
            [(xp.astype(F32) * gk).astype(BF16), (xf * gk).astype(BF16)], axis=0
        )
        v = jnp.concatenate([xp, x], axis=0)
        return h, here, q, qk, k, v, up, gq

    def scores_of(q, k, v, up):
        zero = jnp.zeros((rows, D), BF16)
        right = jnp.concatenate(
            [jnp.concatenate([q, zero], axis=1), jnp.concatenate([zero, up], axis=1)], axis=0
        )
        both = dot(jnp.concatenate([k, v], axis=1), right, NT)
        st = jnp.where(upto, both[rows:, :rows], both[:rows, :rows])
        return st, jnp.where(upto, both[rows:, rows:], both[:rows, rows:])

    def soft(g, h, st, dpt):
        sc = st * (factor * LOG2E) + bias[g, h]
        e = jnp.exp2(sc - jnp.max(sc, axis=0, keepdims=True))
        p = e * (1.0 / jnp.sum(e, axis=0, keepdims=True))
        row_dot = jnp.sum(p * dpt, axis=0, keepdims=True)
        ds = (p * (dpt - row_dot)).astype(BF16)
        sums = jnp.sum(ds.astype(F32), axis=0, keepdims=True)
        return p.astype(BF16), ds, sums

    def compute(step):
        g = step // half_steps
        first = (step % half_steps) * B

        @pl.when(has_prev)
        def _():
            for b in range(B):
                x_copy(g, first + b).wait_recv()

        @pl.when((step == half_steps) & is_last)
        def _():
            t_copy.wait()

        @pl.when((g == 1) & jnp.logical_not(is_last))
        def _():
            for b in range(B):
                d_copy(first + b).wait_recv()

        places = [(first + b, j) for b in range(B) for j in range(G)]
        loaded = [load(g, n, j) for n, j in places]
        raw = [scores_of(q, k, v, up) for _, _, q, _, k, v, up, _ in loaded]
        soft_out = [soft(g, item[0], *both) for item, both in zip(loaded, raw)]
        for (n, _), item, (low, ds, sums) in zip(places, loaded, soft_out):
            h, here, q, qk, k, v, up, gq = item
            left = jnp.concatenate(
                [
                    jnp.concatenate([ds * prev_part, low * prev_part], axis=1),
                    jnp.concatenate([ds * own_part, low * own_part], axis=1),
                ],
                axis=0,
            )
            t = dot(left, jnp.concatenate([qk, up], axis=0), NN)
            turned = ds.T
            ds_t = jnp.concatenate([turned * prev_part_t, turned * own_part_t], axis=1)
            dq = dot(ds_t, k, NN)
            ds_turned = turned.astype(F32)
            all_cols = jnp.sum(ds_turned, axis=0, keepdims=True)
            own_cols = jnp.sum(jnp.where(lane <= sub, ds_turned, 0.0), axis=0, keepdims=True)
            rsend[g, n, :, here] = t[:rows].astype(BF16)
            base[g, n, :, here] = up.astype(F32) + (gq * factor) * dq + t[rows:]
            csend[g, pl.ds(h, 1), :] = all_cols - own_cols
            diff[g, pl.ds(h, 1), :] = sums - own_cols

        for b in range(B):
            n = first + b
            far = edge_high & (n < groups - 1) if relayed else False

            @when(far)
            def _():
                r_far(g, n).start()

            @pl.when(has_prev & jnp.logical_not(far))
            def _():
                r_copy(g, n).start()

        @pl.when(has_prev & (first == groups - B))
        def _():
            c_copy(g).start()

    def finish(step):
        g = step // half_steps
        first = (step % half_steps) * B
        for b in range(B):
            n = first + b

            @pl.when(has_next)
            def _():
                r_copy(g, n).wait_recv()

            total = (base[g, n] + rrecv[g, n].astype(F32)).astype(BF16)
            outs[g, :, lanes(n)] = total

            @pl.when((g == 0) & sends_up)
            def _():
                d_copy(n).start()

            @pl.when(g == 0)
            def _():
                o_copy(0, n).start()

            @pl.when(g == 1)
            def _():
                o_copy(1, n).start()

    def o_copy(g, n):
        to = (o_first, o_second)[g]
        return pltpu.make_async_copy(outs.at[g, :, lanes(n)], to.at[0, :, lanes(n)], o_s.at[g, n])


    def end(step, _):
        finish(step)
        return 0

    def one(step, _):
        compute(step)

        @pl.when((step < half_steps) & jnp.logical_not(edge_low))
        def _():
            for b in range(B):
                send_acts(1, step * B + b)

        @when(edge_low & (step == 0) if relayed else False)
        def _():
            send_some(1, 0, groups)

        @when(passes_on & (core == 1) & (step == 1) if relayed else False)
        def _():
            x_pass_in()

        @when(passes_back & (core == 0) & (step == column + 1) if relayed else False)
        def _():
            r_pass_in()

        early = edge_low & (step < half_steps) if relayed else False

        @pl.when((step >= 1) & (step <= half_steps) & jnp.logical_not(early))
        def _():
            finish(step - 1)

        @when(edge_low & (step == half_steps - 1) if relayed else False)
        def _():
            lax.fori_loop(0, half_steps - 1, end, 0)

        return 0

    lax.fori_loop(0, steps, one, 0)

    @when(passes_back & (core == 1) if relayed else False)
    def _():
        r_pass_in()

    def gates(g):
        @pl.when(has_next)
        def _():
            c_copy(g).wait_recv()

        mask = own_masks[g].astype(F32)
        strict = jnp.where(sub < lane, mask, 0.0)
        forget = dot_exact(diff[g], mask, NT) + dot_exact(crecv[g], strict, NN)
        gate_out[0, g] = forget * jax.nn.sigmoid(-logits[0, g])

    gates(0)

    lax.fori_loop(half_steps, steps, end, 0)
    gates(1)
    put_gates = pltpu.make_async_copy(gate_out, o_gate, g_s)
    put_gates.start()

    @pl.when(has_next)
    def _():
        l_copy.wait_send()

        def go(n):
            x_copy(0, n).wait_send()
            x_copy(1, n).wait_send()

        each_group(go)

    @pl.when(has_prev)
    def _():
        c_copy(0).wait_send()
        c_copy(1).wait_send()

        def go(n):
            r_copy(0, n).wait_send()
            r_copy(1, n).wait_send()

        each_group(go)

    @when(passes_on)
    def _():
        x_pass().wait_send()

    @when(passes_back)
    def _():
        r_pass().wait_send()

    @pl.when(sends_up)
    def _():
        each_group(lambda n: d_copy(n).wait_send())

    def put(n):
        o_copy(0, n).wait()
        o_copy(1, n).wait()

    each_group(put)
    put_gates.wait()


def copy_out(a, b, c, out_a, out_b, out_c, held_a, held_b, held_c, got, put):
    moves = []
    for i, (src, held, dst) in enumerate(
        ((a, held_a, out_a), (b, held_b, out_b), (c, held_c, out_c))
    ):
        moves.append(
            (
                pltpu.make_async_copy(src, held, got.at[i]),
                pltpu.make_async_copy(held, dst, put.at[i]),
            )
        )
    for into, _ in moves:
        into.start()
    for into, out in moves:
        into.wait()
        out.start()
    for _, out in moves:
        out.wait()


def body(sections, shards, acts, out_grad, top_grad, logits, q_gain, k_gain, docs):
    rows = acts.shape[2]
    heads = logits.shape[2]
    groups = heads // G
    anywhere = pl.BlockSpec(memory_space=pl.ANY)
    sem = pltpu.SemaphoreType.DMA
    vmem = pltpu.VMEM
    shapes = (
        jax.ShapeDtypeStruct(out_grad.shape, BF16),
        jax.ShapeDtypeStruct(out_grad.shape, BF16),
        jax.ShapeDtypeStruct(logits.shape, F32),
    )
    results = pl.pallas_call(
        functools.partial(kernel, sections, shards),
        out_shape=shapes,
        in_specs=[anywhere] * 7,
        out_specs=(anywhere,) * 3,
        scratch_shapes=[
            vmem(acts.shape[1:], BF16),
            vmem(logits.shape, F32),
            vmem(q_gain.shape, F32),
            vmem(k_gain.shape, F32),
            vmem(docs.shape, jnp.int32),
            vmem((2, groups, rows, W), BF16),
            vmem(acts.shape[1:], BF16),
            vmem((2, groups, rows, W), BF16),
            vmem((2, groups, rows, W), BF16),
            vmem(acts.shape[1:], BF16),
            vmem(logits.shape, F32),
            vmem((rows, W), BF16),
            vmem((2, heads, rows), F32),
            vmem((2, heads, rows), F32),
            vmem((2, heads, rows), F32),
            vmem((2, heads, rows), F32),
            vmem((2, groups, rows, W), F32),
            vmem((2, heads, rows, rows), F32),
            sem((2, groups)),
            sem((2, groups)),
            sem((2, groups)),
            sem((2, groups)),
            sem((groups,)),
            sem((groups,)),
            sem,
            sem,
            sem,
            sem,
            sem((2,)),
            sem((2,)),
            sem,
            sem((2, groups)),
            sem((7,)),
            sem,
        ],
        compiler_params=pltpu.CompilerParams(
            collective_id=0, has_side_effects=True, vmem_limit_bytes=60 * 1024 * 1024
        ),
    )(acts, out_grad, top_grad, logits, q_gain, k_gain, docs)
    return pl.pallas_call(
        copy_out,
        out_shape=shapes,
        in_specs=[anywhere] * 3,
        out_specs=(anywhere,) * 3,
        scratch_shapes=[vmem(shape.shape, shape.dtype) for shape in shapes]
        + [sem((3,)), sem((3,))],
        compiler_params=pltpu.CompilerParams(vmem_limit_bytes=60 * 1024 * 1024),
    )(*results)


def solution(mesh):
    in_specs = (
        P("section", None, "ctx", None),
        P("section", "ctx", None),
        P("ctx", None),
        P("section", None, None, "ctx"),
        P("section", None),
        P("section", None),
        P("section", None, None),
    )
    out_specs = (
        P("section", "ctx", None),
        P("section", "ctx", None),
        P("section", None, None, "ctx"),
    )
    return jax.shard_map(
        functools.partial(body, mesh.shape["section"], mesh.shape["ctx"]),
        mesh=mesh,
        in_specs=in_specs,
        out_specs=out_specs,
        check_vma=False,
    )
```

```python
import functools
import math

import jax
import jax.numpy as jnp
from jax import lax
from jax.experimental import pallas as pl
from jax.experimental.pallas import tpu as pltpu
from jax.sharding import PartitionSpec as P

MESH = pl.DeviceIdType.MESH
D = 128
G = 4
W = G * D
B = 1
LOG2E = math.log2(math.e)
F32 = jnp.float32
BF16 = jnp.bfloat16
NT = (((1,), (1,)), ((), ()))
NN = (((1,), (0,)), ((), ()))
TN = (((0,), (0,)), ((), ()))


def dot(a, b, dims):
    return lax.dot_general(a, b, dims, preferred_element_type=F32)


def dot_exact(a, b, dims):
    return lax.dot_general(
        a, b, dims, preferred_element_type=F32, precision=lax.Precision.HIGHEST
    )


def kernel(
    sections,
    shards,
    acts,
    out_grad,
    top_grad,
    logits_in,
    q_gain_in,
    k_gain_in,
    docs_in,
    o_first,
    o_second,
    o_gate,
    ownx,
    logits,
    q_gain,
    k_gain,
    docs,
    prevx,
    dy,
    rrecv,
    rsend,
    outs,
    gate_out,
    passing,
    prevlog,
    crecv,
    csend,
    diff,
    base,
    bias,
    x_s,
    x_r,
    r_s,
    r_r,
    d_s,
    d_r,
    f_s,
    f_r,
    l_s,
    l_r,
    c_s,
    c_r,
    y_s,
    o_s,
    in_s,
    g_s,
):
    s = lax.axis_index("section")
    c = lax.axis_index("ctx")
    rows = acts.shape[2]
    heads = logits.shape[2]
    groups = heads // G
    half_steps = groups // B
    steps = 2 * half_steps
    has_prev = c > 0
    has_next = c < shards - 1
    sends_up = s > 0
    is_last = s == sections - 1
    prev_c = lax.rem(c + shards - 1, shards)
    next_c = lax.rem(c + 1, shards)
    prev_s = lax.rem(s + sections - 1, sections)
    next_s = lax.rem(s + 1, sections)

    relayed = shards == 16 and groups == 4
    half = shards // 2
    core = c % 2
    column = (c % half) // 2
    edge_low = (c == half - 1) if relayed else False
    edge_high = (c == half) if relayed else False
    passes_on = (c < half - 2) if relayed else False
    passes_back = (c > half + 1) if relayed else False
    on_relays = [{"ctx": n} for n in range(half - 2)]
    back_relays = [{"ctx": n} for n in range(half + 2, shards)]

    def when(condition):
        return pl.when(condition) if condition is not False else (lambda f: None)

    fetches = [
        pltpu.make_async_copy(logits_in, logits, in_s.at[0]),
        pltpu.make_async_copy(docs_in, docs, in_s.at[1]),
        pltpu.make_async_copy(q_gain_in, q_gain, in_s.at[2]),
        pltpu.make_async_copy(k_gain_in, k_gain, in_s.at[3]),
        pltpu.make_async_copy(acts.at[0, 0], ownx.at[0], in_s.at[4]),
        pltpu.make_async_copy(acts.at[0, 1], ownx.at[1], in_s.at[5]),
        pltpu.make_async_copy(out_grad.at[0], dy.at[0], in_s.at[6]),
    ]
    for i in (4, 0, 1, 2, 3, 6, 5):
        fetches[i].start()

    barrier = pltpu.get_barrier_semaphore()

    def greet(other):
        pl.semaphore_signal(barrier, inc=1, device_id=other, device_id_type=MESH)

    for other in ({"ctx": prev_c}, {"ctx": next_c}, {"section": prev_s}, {"section": next_s}):
        greet(other)

    @when(edge_low)
    def _():
        for other in back_relays:
            greet(other)

    @when(edge_high)
    def _():
        for other in on_relays:
            greet(other)

    @when(passes_on)
    def _():
        greet({"ctx": half - 1})

    @when(passes_back)
    def _():
        greet({"ctx": half})

    def lanes(n):
        return pl.ds(pl.multiple_of(n * W, W), W)

    def remote(src, dst, send, recv, where):
        return pltpu.make_async_remote_copy(
            src_ref=src,
            dst_ref=dst,
            send_sem=send,
            recv_sem=recv,
            device_id=where,
            device_id_type=MESH,
        )

    t_copy = pltpu.make_async_copy(top_grad, dy.at[1], y_s)

    def each_group(f):
        def go(n, _):
            f(n)
            return 0

        lax.fori_loop(0, groups, go, 0)

    @pl.when(is_last)
    def _():
        t_copy.start()

    peers = jnp.int32(4)
    if relayed:
        peers = peers + jnp.where(edge_low, len(on_relays), 0) + jnp.where(edge_high, len(back_relays), 0)
        peers = peers + jnp.where(passes_on | passes_back, 1, 0)
    pl.semaphore_wait(barrier, peers)

    def x_copy(g, n):
        return remote(
            ownx.at[g, :, lanes(n)],
            prevx.at[g, n],
            x_s.at[g, n],
            x_r.at[g, n],
            {"ctx": next_c},
        )

    def x_far(g, n):
        return remote(
            ownx.at[g, :, lanes(n)], passing, x_s.at[g, n], f_r, {"ctx": 2 * n + g}
        )

    def x_pass():
        return remote(
            passing, prevx.at[core, column], f_s, x_r.at[core, column], {"ctx": half}
        )

    def r_copy(g, n):
        return remote(
            rsend.at[g, n], rrecv.at[g, n], r_s.at[g, n], r_r.at[g, n], {"ctx": prev_c}
        )

    def r_far(g, n):
        return remote(rsend.at[g, n], passing, r_s.at[g, n], f_r, {"ctx": half + 2 * n + g})

    def r_pass():
        return remote(
            passing, rrecv.at[core, column], f_s, r_r.at[core, column], {"ctx": half - 1}
        )

    def d_copy(n):
        return remote(
            outs.at[0, :, lanes(n)],
            dy.at[1, :, lanes(n)],
            d_s.at[n],
            d_r.at[n],
            {"section": prev_s},
        )

    def c_copy(g):
        return remote(csend.at[g], crecv.at[g], c_s.at[g], c_r.at[g], {"ctx": prev_c})

    l_copy = remote(logits.at[0], prevlog, l_s, l_r, {"ctx": next_c})

    def x_pass_in():
        x_far(0, 0).wait_recv()
        x_pass().start()

    def r_pass_in():
        r_far(0, 0).wait_recv()
        r_pass().start()

    def send_acts(g, n):
        far = edge_low & (n < groups - 1) if relayed else False

        @when(far)
        def _():
            x_far(g, n).start()

        @pl.when(has_next & jnp.logical_not(far))
        def _():
            x_copy(g, n).start()

    def send_some(g, begin, stop):
        def go(n, _):
            send_acts(g, n)
            return 0

        lax.fori_loop(begin, stop, go, 0)

    fetches[0].wait()
    fetches[4].wait()

    @pl.when(has_next)
    def _():
        l_copy.start()

    send_some(0, 0, groups // 2)

    @pl.when(jnp.logical_not(has_prev))
    def _():
        prevx[...] = jnp.zeros_like(prevx)
        prevlog[...] = jnp.zeros_like(prevlog)

    @pl.when(jnp.logical_not(has_next))
    def _():
        rrecv[...] = jnp.zeros_like(rrecv)
        crecv[...] = jnp.zeros_like(crecv)

    for i in (1, 2, 3, 6, 5):
        fetches[i].wait()

    def log_forget(x):
        return jnp.minimum(x, 0.0) - jnp.log1p(jnp.exp(-jnp.abs(x)))

    sub = lax.broadcasted_iota(jnp.int32, (rows, rows), 0)
    lane = lax.broadcasted_iota(jnp.int32, (rows, rows), 1)
    anchor = (c * rows).astype(F32)
    own_masks = []
    prev_masks = []
    n_docs = docs.shape[2]
    for g in range(2):
        d0 = lax.broadcasted_iota(jnp.int32, (n_docs, n_docs), 0)
        d1 = lax.broadcasted_iota(jnp.int32, (n_docs, n_docs), 1)
        lengths = docs[0, g : g + 1, :].astype(F32)
        bounds = jnp.sum(jnp.where(d1 <= d0, lengths, 0.0), axis=1, keepdims=True)
        pos = lax.broadcasted_iota(jnp.int32, (n_docs, rows), 1).astype(F32) + anchor
        begin = jnp.max(jnp.where(bounds <= pos, bounds, 0.0), axis=0, keepdims=True)
        key_pos = sub.astype(F32) + anchor
        own_masks.append((key_pos >= begin) & (sub <= lane))
        prev_masks.append((key_pos - float(rows) >= begin) & (sub > lane))

    @pl.when(has_prev)
    def _():
        l_copy.wait_recv()

    def make_bias(g):
        upto = (lane <= sub).astype(F32)
        after = (lane > sub).astype(F32)
        own = dot_exact(upto, log_forget(logits[0, g]), NT) * LOG2E
        before = dot_exact(after, log_forget(prevlog[g]), NT) * -LOG2E
        for h in range(heads):
            bias[g, h] = jnp.where(
                own_masks[g],
                -own[:, h : h + 1],
                jnp.where(prev_masks[g], -before[:, h : h + 1], -1e30),
            )

    make_bias(0)
    send_some(0, groups // 2, groups)

    @when(passes_on & (core == 0) if relayed else False)
    def _():
        x_pass_in()

    make_bias(1)
    factor = 1.0 / math.sqrt(D)
    upto = sub <= lane
    own_part = upto.astype(F32).astype(BF16)
    prev_part = (sub > lane).astype(F32).astype(BF16)
    own_part_t = (lane <= sub).astype(F32).astype(BF16)
    prev_part_t = (lane > sub).astype(F32).astype(BF16)

    def load(g, n, j):
        h = n * G + j
        col = pl.ds(pl.multiple_of(h * D, D), D)
        here = slice(j * D, (j + 1) * D)
        x = ownx[g, :, col]
        xp = prevx[g, n, :, here]
        up = dy[g, :, col]
        gq = q_gain[:, col]
        gk = k_gain[:, col]
        xf = x.astype(F32)
        q = (xf * gq).astype(BF16)
        qk = (q.astype(F32) * (gk * factor)).astype(BF16)
        k = jnp.concatenate(
            [(xp.astype(F32) * gk).astype(BF16), (xf * gk).astype(BF16)], axis=0
        )
        v = jnp.concatenate([xp, x], axis=0)
        return h, here, q, qk, k, v, up, gq

    def scores_of(q, k, v, up):
        zero = jnp.zeros((rows, D), BF16)
        right = jnp.concatenate(
            [jnp.concatenate([q, zero], axis=1), jnp.concatenate([zero, up], axis=1)], axis=0
        )
        both = dot(jnp.concatenate([k, v], axis=1), right, NT)
        st = jnp.where(upto, both[rows:, :rows], both[:rows, :rows])
        return st, jnp.where(upto, both[rows:, rows:], both[:rows, rows:])

    def soft(g, h, st, dpt):
        sc = st * (factor * LOG2E) + bias[g, h]
        e = jnp.exp2(sc - jnp.max(sc, axis=0, keepdims=True))
        p = e * (1.0 / jnp.sum(e, axis=0, keepdims=True))
        row_dot = jnp.sum(p * dpt, axis=0, keepdims=True)
        ds = (p * (dpt - row_dot)).astype(BF16)
        sums = jnp.sum(ds.astype(F32), axis=0, keepdims=True)
        return p.astype(BF16), ds, sums

    def compute(step):
        g = step // half_steps
        first = (step % half_steps) * B

        @pl.when(has_prev)
        def _():
            for b in range(B):
                x_copy(g, first + b).wait_recv()

        @pl.when((step == half_steps) & is_last)
        def _():
            t_copy.wait()

        @pl.when((g == 1) & jnp.logical_not(is_last))
        def _():
            for b in range(B):
                d_copy(first + b).wait_recv()

        places = [(first + b, j) for b in range(B) for j in range(G)]
        loaded = [load(g, n, j) for n, j in places]
        raw = [scores_of(q, k, v, up) for _, _, q, _, k, v, up, _ in loaded]
        soft_out = [soft(g, item[0], *both) for item, both in zip(loaded, raw)]
        for (n, _), item, (low, ds, sums) in zip(places, loaded, soft_out):
            h, here, q, qk, k, v, up, gq = item
            left = jnp.concatenate(
                [
                    jnp.concatenate([ds * prev_part, low * prev_part], axis=1),
                    jnp.concatenate([ds * own_part, low * own_part], axis=1),
                ],
                axis=0,
            )
            t = dot(left, jnp.concatenate([qk, up], axis=0), NN)
            turned = ds.T
            ds_t = jnp.concatenate([turned * prev_part_t, turned * own_part_t], axis=1)
            dq = dot(ds_t, k, NN)
            ds_turned = turned.astype(F32)
            all_cols = jnp.sum(ds_turned, axis=0, keepdims=True)
            own_cols = jnp.sum(jnp.where(lane <= sub, ds_turned, 0.0), axis=0, keepdims=True)
            rsend[g, n, :, here] = t[:rows].astype(BF16)
            base[g, n, :, here] = up.astype(F32) + (gq * factor) * dq + t[rows:]
            csend[g, pl.ds(h, 1), :] = all_cols - own_cols
            diff[g, pl.ds(h, 1), :] = sums - own_cols

        for b in range(B):
            n = first + b
            far = edge_high & (n > 0) if relayed else False

            @when(far)
            def _():
                r_far(g, n).start()

            @pl.when(has_prev & jnp.logical_not(far))
            def _():
                r_copy(g, n).start()

        @pl.when(has_prev & (first == groups - B))
        def _():
            c_copy(g).start()

    def finish(step):
        g = step // half_steps
        first = (step % half_steps) * B
        for b in range(B):
            n = first + b

            @pl.when(has_next)
            def _():
                r_copy(g, n).wait_recv()

            total = (base[g, n] + rrecv[g, n].astype(F32)).astype(BF16)
            outs[g, :, lanes(n)] = total

            @pl.when((g == 0) & sends_up)
            def _():
                d_copy(n).start()

            @pl.when(g == 0)
            def _():
                o_copy(0, n).start()

            @pl.when(g == 1)
            def _():
                o_copy(1, n).start()

    def o_copy(g, n):
        to = (o_first, o_second)[g]
        return pltpu.make_async_copy(outs.at[g, :, lanes(n)], to.at[0, :, lanes(n)], o_s.at[g, n])


    def end(step, _):
        finish(step)
        return 0

    def one(step, _):
        compute(step)

        @pl.when((step < half_steps) & jnp.logical_not(edge_low))
        def _():
            for b in range(B):
                send_acts(1, step * B + b)

        @when(edge_low & (step == 0) if relayed else False)
        def _():
            send_some(1, 0, groups)

        @when(passes_on & (core == 1) & (step == 1) if relayed else False)
        def _():
            x_pass_in()

        @when(passes_back & (core == 0) & (step == column + 3) if relayed else False)
        def _():
            r_pass_in()

        early = edge_low & (step <= half_steps) if relayed else False

        @pl.when((step >= 1) & (step <= half_steps) & jnp.logical_not(early))
        def _():
            finish(step - 1)

        @when(edge_low & (step == half_steps - 1) if relayed else False)
        def _():
            lax.fori_loop(0, half_steps, end, 0)

        return 0

    lax.fori_loop(0, steps, one, 0)

    @when(passes_back & (core == 1) if relayed else False)
    def _():
        r_pass_in()

    def gates(g):
        @pl.when(has_next)
        def _():
            c_copy(g).wait_recv()

        mask = own_masks[g].astype(F32)
        strict = jnp.where(sub < lane, mask, 0.0)
        forget = dot_exact(diff[g], mask, NT) + dot_exact(crecv[g], strict, NN)
        gate_out[0, g] = forget * jax.nn.sigmoid(-logits[0, g])

    gates(0)

    lax.fori_loop(half_steps, steps, end, 0)
    gates(1)
    put_gates = pltpu.make_async_copy(gate_out, o_gate, g_s)
    put_gates.start()

    @pl.when(has_next)
    def _():
        l_copy.wait_send()

        def go(n):
            x_copy(0, n).wait_send()
            x_copy(1, n).wait_send()

        each_group(go)

    @pl.when(has_prev)
    def _():
        c_copy(0).wait_send()
        c_copy(1).wait_send()

        def go(n):
            r_copy(0, n).wait_send()
            r_copy(1, n).wait_send()

        each_group(go)

    @when(passes_on)
    def _():
        x_pass().wait_send()

    @when(passes_back)
    def _():
        r_pass().wait_send()

    @pl.when(sends_up)
    def _():
        each_group(lambda n: d_copy(n).wait_send())

    def put(n):
        o_copy(0, n).wait()
        o_copy(1, n).wait()

    each_group(put)
    put_gates.wait()


def copy_out(a, b, c, out_a, out_b, out_c, held_a, held_b, held_c, got, put):
    moves = []
    for i, (src, held, dst) in enumerate(
        ((a, held_a, out_a), (b, held_b, out_b), (c, held_c, out_c))
    ):
        moves.append(
            (
                pltpu.make_async_copy(src, held, got.at[i]),
                pltpu.make_async_copy(held, dst, put.at[i]),
            )
        )
    for into, _ in moves:
        into.start()
    for into, out in moves:
        into.wait()
        out.start()
    for _, out in moves:
        out.wait()


def body(sections, shards, acts, out_grad, top_grad, logits, q_gain, k_gain, docs):
    rows = acts.shape[2]
    heads = logits.shape[2]
    groups = heads // G
    anywhere = pl.BlockSpec(memory_space=pl.ANY)
    sem = pltpu.SemaphoreType.DMA
    vmem = pltpu.VMEM
    shapes = (
        jax.ShapeDtypeStruct(out_grad.shape, BF16),
        jax.ShapeDtypeStruct(out_grad.shape, BF16),
        jax.ShapeDtypeStruct(logits.shape, F32),
    )
    results = pl.pallas_call(
        functools.partial(kernel, sections, shards),
        out_shape=shapes,
        in_specs=[anywhere] * 7,
        out_specs=(anywhere,) * 3,
        scratch_shapes=[
            vmem(acts.shape[1:], BF16),
            vmem(logits.shape, F32),
            vmem(q_gain.shape, F32),
            vmem(k_gain.shape, F32),
            vmem(docs.shape, jnp.int32),
            vmem((2, groups, rows, W), BF16),
            vmem(acts.shape[1:], BF16),
            vmem((2, groups, rows, W), BF16),
            vmem((2, groups, rows, W), BF16),
            vmem(acts.shape[1:], BF16),
            vmem(logits.shape, F32),
            vmem((rows, W), BF16),
            vmem((2, heads, rows), F32),
            vmem((2, heads, rows), F32),
            vmem((2, heads, rows), F32),
            vmem((2, heads, rows), F32),
            vmem((2, groups, rows, W), F32),
            vmem((2, heads, rows, rows), F32),
            sem((2, groups)),
            sem((2, groups)),
            sem((2, groups)),
            sem((2, groups)),
            sem((groups,)),
            sem((groups,)),
            sem,
            sem,
            sem,
            sem,
            sem((2,)),
            sem((2,)),
            sem,
            sem((2, groups)),
            sem((7,)),
            sem,
        ],
        compiler_params=pltpu.CompilerParams(
            collective_id=0, has_side_effects=True, vmem_limit_bytes=60 * 1024 * 1024
        ),
    )(acts, out_grad, top_grad, logits, q_gain, k_gain, docs)
    return pl.pallas_call(
        copy_out,
        out_shape=shapes,
        in_specs=[anywhere] * 3,
        out_specs=(anywhere,) * 3,
        scratch_shapes=[vmem(shape.shape, shape.dtype) for shape in shapes]
        + [sem((3,)), sem((3,))],
        compiler_params=pltpu.CompilerParams(vmem_limit_bytes=60 * 1024 * 1024),
    )(*results)


def solution(mesh):
    in_specs = (
        P("section", None, "ctx", None),
        P("section", "ctx", None),
        P("ctx", None),
        P("section", None, None, "ctx"),
        P("section", None),
        P("section", None),
        P("section", None, None),
    )
    out_specs = (
        P("section", "ctx", None),
        P("section", "ctx", None),
        P("section", None, None, "ctx"),
    )
    return jax.shard_map(
        functools.partial(body, mesh.shape["section"], mesh.shape["ctx"]),
        mesh=mesh,
        in_specs=in_specs,
        out_specs=out_specs,
        check_vma=False,
    )
```

```python
import functools
import math

import jax
import jax.numpy as jnp
from jax import lax
from jax.experimental import pallas as pl
from jax.experimental.pallas import tpu as pltpu
from jax.sharding import PartitionSpec as P

MESH = pl.DeviceIdType.MESH
D = 128
G = 4
W = G * D
B = 1
LOG2E = math.log2(math.e)
F32 = jnp.float32
BF16 = jnp.bfloat16
NT = (((1,), (1,)), ((), ()))
NN = (((1,), (0,)), ((), ()))
TN = (((0,), (0,)), ((), ()))


def dot(a, b, dims):
    return lax.dot_general(a, b, dims, preferred_element_type=F32)


def dot_exact(a, b, dims):
    return lax.dot_general(
        a, b, dims, preferred_element_type=F32, precision=lax.Precision.HIGHEST
    )


def kernel(
    sections,
    shards,
    acts,
    out_grad,
    top_grad,
    logits_in,
    q_gain_in,
    k_gain_in,
    docs_in,
    o_first,
    o_second,
    o_gate,
    ownx,
    logits,
    q_gain,
    k_gain,
    docs,
    prevx,
    dy,
    rrecv,
    rsend,
    outs,
    gate_out,
    passing,
    prevlog,
    crecv,
    csend,
    diff,
    base,
    bias,
    x_s,
    x_r,
    r_s,
    r_r,
    d_s,
    d_r,
    f_s,
    f_r,
    l_s,
    l_r,
    c_s,
    c_r,
    y_s,
    o_s,
    in_s,
    g_s,
):
    s = lax.axis_index("section")
    c = lax.axis_index("ctx")
    rows = acts.shape[2]
    heads = logits.shape[2]
    groups = heads // G
    half_steps = groups // B
    steps = 2 * half_steps
    has_prev = c > 0
    has_next = c < shards - 1
    sends_up = s > 0
    is_last = s == sections - 1
    prev_c = lax.rem(c + shards - 1, shards)
    next_c = lax.rem(c + 1, shards)
    prev_s = lax.rem(s + sections - 1, sections)
    next_s = lax.rem(s + 1, sections)

    relayed = shards == 16 and groups == 4
    half = shards // 2
    core = c % 2
    column = (c % half) // 2
    edge_low = (c == half - 1) if relayed else False
    edge_high = (c == half) if relayed else False
    passes_on = (c < half - 2) if relayed else False
    passes_back = (c > half + 1) & (core == 0) if relayed else False
    on_relays = [{"ctx": n} for n in range(half - 2)]
    back_relays = [{"ctx": n} for n in range(half + 2, shards, 2)]

    def when(condition):
        return pl.when(condition) if condition is not False else (lambda f: None)

    fetches = [
        pltpu.make_async_copy(logits_in, logits, in_s.at[0]),
        pltpu.make_async_copy(docs_in, docs, in_s.at[1]),
        pltpu.make_async_copy(q_gain_in, q_gain, in_s.at[2]),
        pltpu.make_async_copy(k_gain_in, k_gain, in_s.at[3]),
        pltpu.make_async_copy(acts.at[0, 0], ownx.at[0], in_s.at[4]),
        pltpu.make_async_copy(acts.at[0, 1], ownx.at[1], in_s.at[5]),
        pltpu.make_async_copy(out_grad.at[0], dy.at[0], in_s.at[6]),
    ]
    for i in (4, 0, 1, 2, 3, 6, 5):
        fetches[i].start()

    barrier = pltpu.get_barrier_semaphore()

    def greet(other):
        pl.semaphore_signal(barrier, inc=1, device_id=other, device_id_type=MESH)

    for other in ({"ctx": prev_c}, {"ctx": next_c}, {"section": prev_s}, {"section": next_s}):
        greet(other)

    @when(edge_low)
    def _():
        for other in back_relays:
            greet(other)

    @when(edge_high)
    def _():
        for other in on_relays:
            greet(other)

    @when(passes_on)
    def _():
        greet({"ctx": half - 1})

    @when(passes_back)
    def _():
        greet({"ctx": half})

    def lanes(n):
        return pl.ds(pl.multiple_of(n * W, W), W)

    def remote(src, dst, send, recv, where):
        return pltpu.make_async_remote_copy(
            src_ref=src,
            dst_ref=dst,
            send_sem=send,
            recv_sem=recv,
            device_id=where,
            device_id_type=MESH,
        )

    t_copy = pltpu.make_async_copy(top_grad, dy.at[1], y_s)

    def each_group(f):
        def go(n, _):
            f(n)
            return 0

        lax.fori_loop(0, groups, go, 0)

    @pl.when(is_last)
    def _():
        t_copy.start()

    peers = jnp.int32(4)
    if relayed:
        peers = peers + jnp.where(edge_low, len(on_relays), 0) + jnp.where(edge_high, len(back_relays), 0)
        peers = peers + jnp.where(passes_on | passes_back, 1, 0)
    pl.semaphore_wait(barrier, peers)

    def x_copy(g, n):
        return remote(
            ownx.at[g, :, lanes(n)],
            prevx.at[g, n],
            x_s.at[g, n],
            x_r.at[g, n],
            {"ctx": next_c},
        )

    def x_far(g, n):
        return remote(
            ownx.at[g, :, lanes(n)], passing, x_s.at[g, n], f_r, {"ctx": 2 * n + g}
        )

    def x_pass():
        return remote(
            passing, prevx.at[core, column], f_s, x_r.at[core, column], {"ctx": half}
        )

    def r_copy(g, n):
        return remote(
            rsend.at[g, n], rrecv.at[g, n], r_s.at[g, n], r_r.at[g, n], {"ctx": prev_c}
        )

    def r_far(g, n):
        return remote(rsend.at[g, n], passing, r_s.at[g, n], f_r, {"ctx": half + 2 * n + g})

    def r_pass():
        return remote(
            passing, rrecv.at[core, column], f_s, r_r.at[core, column], {"ctx": half - 1}
        )

    def d_copy(n):
        return remote(
            outs.at[0, :, lanes(n)],
            dy.at[1, :, lanes(n)],
            d_s.at[n],
            d_r.at[n],
            {"section": prev_s},
        )

    def c_copy(g):
        return remote(csend.at[g], crecv.at[g], c_s.at[g], c_r.at[g], {"ctx": prev_c})

    l_copy = remote(logits.at[0], prevlog, l_s, l_r, {"ctx": next_c})

    def x_pass_in():
        x_far(0, 0).wait_recv()
        x_pass().start()

    def r_pass_in():
        r_far(0, 0).wait_recv()
        r_pass().start()

    def send_acts(g, n):
        far = edge_low & (n < groups - 1) if relayed else False

        @when(far)
        def _():
            x_far(g, n).start()

        @pl.when(has_next & jnp.logical_not(far))
        def _():
            x_copy(g, n).start()

    def send_some(g, begin, stop):
        def go(n, _):
            send_acts(g, n)
            return 0

        lax.fori_loop(begin, stop, go, 0)

    fetches[0].wait()
    fetches[4].wait()

    @pl.when(has_next)
    def _():
        l_copy.start()

    send_some(0, 0, groups // 2)

    @pl.when(jnp.logical_not(has_prev))
    def _():
        prevx[...] = jnp.zeros_like(prevx)
        prevlog[...] = jnp.zeros_like(prevlog)

    @pl.when(jnp.logical_not(has_next))
    def _():
        rrecv[...] = jnp.zeros_like(rrecv)
        crecv[...] = jnp.zeros_like(crecv)

    for i in (1, 2, 3, 6, 5):
        fetches[i].wait()

    def log_forget(x):
        return jnp.minimum(x, 0.0) - jnp.log1p(jnp.exp(-jnp.abs(x)))

    sub = lax.broadcasted_iota(jnp.int32, (rows, rows), 0)
    lane = lax.broadcasted_iota(jnp.int32, (rows, rows), 1)
    anchor = (c * rows).astype(F32)
    own_masks = []
    prev_masks = []
    n_docs = docs.shape[2]
    for g in range(2):
        d0 = lax.broadcasted_iota(jnp.int32, (n_docs, n_docs), 0)
        d1 = lax.broadcasted_iota(jnp.int32, (n_docs, n_docs), 1)
        lengths = docs[0, g : g + 1, :].astype(F32)
        bounds = jnp.sum(jnp.where(d1 <= d0, lengths, 0.0), axis=1, keepdims=True)
        pos = lax.broadcasted_iota(jnp.int32, (n_docs, rows), 1).astype(F32) + anchor
        begin = jnp.max(jnp.where(bounds <= pos, bounds, 0.0), axis=0, keepdims=True)
        key_pos = sub.astype(F32) + anchor
        own_masks.append((key_pos >= begin) & (sub <= lane))
        prev_masks.append((key_pos - float(rows) >= begin) & (sub > lane))

    @pl.when(has_prev)
    def _():
        l_copy.wait_recv()

    def make_bias(g):
        upto = (lane <= sub).astype(F32)
        after = (lane > sub).astype(F32)
        own = dot_exact(upto, log_forget(logits[0, g]), NT) * LOG2E
        before = dot_exact(after, log_forget(prevlog[g]), NT) * -LOG2E
        for h in range(heads):
            bias[g, h] = jnp.where(
                own_masks[g],
                -own[:, h : h + 1],
                jnp.where(prev_masks[g], -before[:, h : h + 1], -1e30),
            )

    make_bias(0)
    send_some(0, groups // 2, groups)

    @when(passes_on & (core == 0) if relayed else False)
    def _():
        x_pass_in()

    make_bias(1)
    factor = 1.0 / math.sqrt(D)
    upto = sub <= lane
    own_part = upto.astype(F32).astype(BF16)
    prev_part = (sub > lane).astype(F32).astype(BF16)
    own_part_t = (lane <= sub).astype(F32).astype(BF16)
    prev_part_t = (lane > sub).astype(F32).astype(BF16)

    def load(g, n, j):
        h = n * G + j
        col = pl.ds(pl.multiple_of(h * D, D), D)
        here = slice(j * D, (j + 1) * D)
        x = ownx[g, :, col]
        xp = prevx[g, n, :, here]
        up = dy[g, :, col]
        gq = q_gain[:, col]
        gk = k_gain[:, col]
        xf = x.astype(F32)
        q = (xf * gq).astype(BF16)
        qk = (q.astype(F32) * (gk * factor)).astype(BF16)
        k = jnp.concatenate(
            [(xp.astype(F32) * gk).astype(BF16), (xf * gk).astype(BF16)], axis=0
        )
        v = jnp.concatenate([xp, x], axis=0)
        return h, here, q, qk, k, v, up, gq

    def scores_of(q, k, v, up):
        zero = jnp.zeros((rows, D), BF16)
        right = jnp.concatenate(
            [jnp.concatenate([q, zero], axis=1), jnp.concatenate([zero, up], axis=1)], axis=0
        )
        both = dot(jnp.concatenate([k, v], axis=1), right, NT)
        st = jnp.where(upto, both[rows:, :rows], both[:rows, :rows])
        return st, jnp.where(upto, both[rows:, rows:], both[:rows, rows:])

    def soft(g, h, st, dpt):
        sc = st * (factor * LOG2E) + bias[g, h]
        e = jnp.exp2(sc - jnp.max(sc, axis=0, keepdims=True))
        p = e * (1.0 / jnp.sum(e, axis=0, keepdims=True))
        row_dot = jnp.sum(p * dpt, axis=0, keepdims=True)
        ds = (p * (dpt - row_dot)).astype(BF16)
        sums = jnp.sum(ds.astype(F32), axis=0, keepdims=True)
        return p.astype(BF16), ds, sums

    def compute(step):
        g = step // half_steps
        first = (step % half_steps) * B

        @pl.when(has_prev)
        def _():
            for b in range(B):
                x_copy(g, first + b).wait_recv()

        @pl.when((step == half_steps) & is_last)
        def _():
            t_copy.wait()

        @pl.when((g == 1) & jnp.logical_not(is_last))
        def _():
            for b in range(B):
                d_copy(first + b).wait_recv()

        places = [(first + b, j) for b in range(B) for j in range(G)]
        loaded = [load(g, n, j) for n, j in places]
        raw = [scores_of(q, k, v, up) for _, _, q, _, k, v, up, _ in loaded]
        soft_out = [soft(g, item[0], *both) for item, both in zip(loaded, raw)]
        for (n, _), item, (low, ds, sums) in zip(places, loaded, soft_out):
            h, here, q, qk, k, v, up, gq = item
            left = jnp.concatenate(
                [
                    jnp.concatenate([ds * prev_part, low * prev_part], axis=1),
                    jnp.concatenate([ds * own_part, low * own_part], axis=1),
                ],
                axis=0,
            )
            t = dot(left, jnp.concatenate([qk, up], axis=0), NN)
            turned = ds.T
            ds_t = jnp.concatenate([turned * prev_part_t, turned * own_part_t], axis=1)
            dq = dot(ds_t, k, NN)
            ds_turned = turned.astype(F32)
            all_cols = jnp.sum(ds_turned, axis=0, keepdims=True)
            own_cols = jnp.sum(jnp.where(lane <= sub, ds_turned, 0.0), axis=0, keepdims=True)
            rsend[g, n, :, here] = t[:rows].astype(BF16)
            base[g, n, :, here] = up.astype(F32) + (gq * factor) * dq + t[rows:]
            csend[g, pl.ds(h, 1), :] = all_cols - own_cols
            diff[g, pl.ds(h, 1), :] = sums - own_cols

        for b in range(B):
            n = first + b
            far = edge_high & (g == 0) & (n > 0) if relayed else False

            @when(far)
            def _():
                r_far(g, n).start()

            @pl.when(has_prev & jnp.logical_not(far))
            def _():
                r_copy(g, n).start()

        @pl.when(has_prev & (first == groups - B))
        def _():
            c_copy(g).start()

    def finish(step):
        g = step // half_steps
        first = (step % half_steps) * B
        for b in range(B):
            n = first + b

            @pl.when(has_next)
            def _():
                r_copy(g, n).wait_recv()

            total = (base[g, n] + rrecv[g, n].astype(F32)).astype(BF16)
            outs[g, :, lanes(n)] = total

            @pl.when((g == 0) & sends_up)
            def _():
                d_copy(n).start()

            @pl.when(g == 0)
            def _():
                o_copy(0, n).start()

            @pl.when(g == 1)
            def _():
                o_copy(1, n).start()

    def o_copy(g, n):
        to = (o_first, o_second)[g]
        return pltpu.make_async_copy(outs.at[g, :, lanes(n)], to.at[0, :, lanes(n)], o_s.at[g, n])


    def end(step, _):
        finish(step)
        return 0

    def one(step, _):
        compute(step)

        @pl.when((step < half_steps) & jnp.logical_not(edge_low))
        def _():
            for b in range(B):
                send_acts(1, step * B + b)

        @when(edge_low & (step == 0) if relayed else False)
        def _():
            send_some(1, 0, groups)

        @when(passes_on & (core == 1) & (step == 1) if relayed else False)
        def _():
            x_pass_in()

        @when(passes_back & (step == column + 3) if relayed else False)
        def _():
            r_pass_in()

        early = edge_low & (step <= half_steps) if relayed else False

        @pl.when((step >= 1) & (step <= half_steps) & jnp.logical_not(early))
        def _():
            finish(step - 1)

        @when(edge_low & (step == half_steps - 1) if relayed else False)
        def _():
            lax.fori_loop(0, half_steps, end, 0)

        return 0

    lax.fori_loop(0, steps, one, 0)

    def gates(g):
        @pl.when(has_next)
        def _():
            c_copy(g).wait_recv()

        mask = own_masks[g].astype(F32)
        strict = jnp.where(sub < lane, mask, 0.0)
        forget = dot_exact(diff[g], mask, NT) + dot_exact(crecv[g], strict, NN)
        gate_out[0, g] = forget * jax.nn.sigmoid(-logits[0, g])

    gates(0)

    lax.fori_loop(half_steps, steps, end, 0)
    gates(1)
    put_gates = pltpu.make_async_copy(gate_out, o_gate, g_s)
    put_gates.start()

    @pl.when(has_next)
    def _():
        l_copy.wait_send()

        def go(n):
            x_copy(0, n).wait_send()
            x_copy(1, n).wait_send()

        each_group(go)

    @pl.when(has_prev)
    def _():
        c_copy(0).wait_send()
        c_copy(1).wait_send()

        def go(n):
            r_copy(0, n).wait_send()
            r_copy(1, n).wait_send()

        each_group(go)

    @when(passes_on)
    def _():
        x_pass().wait_send()

    @when(passes_back)
    def _():
        r_pass().wait_send()

    @pl.when(sends_up)
    def _():
        each_group(lambda n: d_copy(n).wait_send())

    def put(n):
        o_copy(0, n).wait()
        o_copy(1, n).wait()

    each_group(put)
    put_gates.wait()


def copy_out(a, b, c, out_a, out_b, out_c, held_a, held_b, held_c, got, put):
    moves = []
    for i, (src, held, dst) in enumerate(
        ((a, held_a, out_a), (b, held_b, out_b), (c, held_c, out_c))
    ):
        moves.append(
            (
                pltpu.make_async_copy(src, held, got.at[i]),
                pltpu.make_async_copy(held, dst, put.at[i]),
            )
        )
    for into, _ in moves:
        into.start()
    for into, out in moves:
        into.wait()
        out.start()
    for _, out in moves:
        out.wait()


def body(sections, shards, acts, out_grad, top_grad, logits, q_gain, k_gain, docs):
    rows = acts.shape[2]
    heads = logits.shape[2]
    groups = heads // G
    anywhere = pl.BlockSpec(memory_space=pl.ANY)
    sem = pltpu.SemaphoreType.DMA
    vmem = pltpu.VMEM
    shapes = (
        jax.ShapeDtypeStruct(out_grad.shape, BF16),
        jax.ShapeDtypeStruct(out_grad.shape, BF16),
        jax.ShapeDtypeStruct(logits.shape, F32),
    )
    results = pl.pallas_call(
        functools.partial(kernel, sections, shards),
        out_shape=shapes,
        in_specs=[anywhere] * 7,
        out_specs=(anywhere,) * 3,
        scratch_shapes=[
            vmem(acts.shape[1:], BF16),
            vmem(logits.shape, F32),
            vmem(q_gain.shape, F32),
            vmem(k_gain.shape, F32),
            vmem(docs.shape, jnp.int32),
            vmem((2, groups, rows, W), BF16),
            vmem(acts.shape[1:], BF16),
            vmem((2, groups, rows, W), BF16),
            vmem((2, groups, rows, W), BF16),
            vmem(acts.shape[1:], BF16),
            vmem(logits.shape, F32),
            vmem((rows, W), BF16),
            vmem((2, heads, rows), F32),
            vmem((2, heads, rows), F32),
            vmem((2, heads, rows), F32),
            vmem((2, heads, rows), F32),
            vmem((2, groups, rows, W), F32),
            vmem((2, heads, rows, rows), F32),
            sem((2, groups)),
            sem((2, groups)),
            sem((2, groups)),
            sem((2, groups)),
            sem((groups,)),
            sem((groups,)),
            sem,
            sem,
            sem,
            sem,
            sem((2,)),
            sem((2,)),
            sem,
            sem((2, groups)),
            sem((7,)),
            sem,
        ],
        compiler_params=pltpu.CompilerParams(
            collective_id=0, has_side_effects=True, vmem_limit_bytes=60 * 1024 * 1024
        ),
    )(acts, out_grad, top_grad, logits, q_gain, k_gain, docs)
    return pl.pallas_call(
        copy_out,
        out_shape=shapes,
        in_specs=[anywhere] * 3,
        out_specs=(anywhere,) * 3,
        scratch_shapes=[vmem(shape.shape, shape.dtype) for shape in shapes]
        + [sem((3,)), sem((3,))],
        compiler_params=pltpu.CompilerParams(vmem_limit_bytes=60 * 1024 * 1024),
    )(*results)


def solution(mesh):
    in_specs = (
        P("section", None, "ctx", None),
        P("section", "ctx", None),
        P("ctx", None),
        P("section", None, None, "ctx"),
        P("section", None),
        P("section", None),
        P("section", None, None),
    )
    out_specs = (
        P("section", "ctx", None),
        P("section", "ctx", None),
        P("section", None, None, "ctx"),
    )
    return jax.shard_map(
        functools.partial(body, mesh.shape["section"], mesh.shape["ctx"]),
        mesh=mesh,
        in_specs=in_specs,
        out_specs=out_specs,
        check_vma=False,
    )
```

```python
import functools
import math

import jax
import jax.numpy as jnp
from jax import lax
from jax.experimental import pallas as pl
from jax.experimental.pallas import tpu as pltpu
from jax.sharding import PartitionSpec as P

MESH = pl.DeviceIdType.MESH
D = 128
G = 4
W = G * D
B = 1
LOG2E = math.log2(math.e)
F32 = jnp.float32
BF16 = jnp.bfloat16
NT = (((1,), (1,)), ((), ()))
NN = (((1,), (0,)), ((), ()))
TN = (((0,), (0,)), ((), ()))


def dot(a, b, dims):
    return lax.dot_general(a, b, dims, preferred_element_type=F32)


def dot_exact(a, b, dims):
    return lax.dot_general(
        a, b, dims, preferred_element_type=F32, precision=lax.Precision.HIGHEST
    )


def kernel(
    sections,
    shards,
    acts,
    out_grad,
    top_grad,
    logits_in,
    q_gain_in,
    k_gain_in,
    docs_in,
    o_first,
    o_second,
    o_gate,
    ownx,
    logits,
    q_gain,
    k_gain,
    docs,
    prevx,
    dy,
    rrecv,
    rsend,
    outs,
    gate_out,
    passing,
    prevlog,
    crecv,
    csend,
    diff,
    base,
    bias,
    x_s,
    x_r,
    r_s,
    r_r,
    d_s,
    d_r,
    f_s,
    f_r,
    l_s,
    l_r,
    c_s,
    c_r,
    y_s,
    o_s,
    in_s,
    g_s,
):
    s = lax.axis_index("section")
    c = lax.axis_index("ctx")
    rows = acts.shape[2]
    heads = logits.shape[2]
    groups = heads // G
    half_steps = groups // B
    steps = 2 * half_steps
    has_prev = c > 0
    has_next = c < shards - 1
    sends_up = s > 0
    is_last = s == sections - 1
    prev_c = lax.rem(c + shards - 1, shards)
    next_c = lax.rem(c + 1, shards)
    prev_s = lax.rem(s + sections - 1, sections)
    next_s = lax.rem(s + 1, sections)

    relayed = shards == 16 and groups == 4
    half = shards // 2
    core = c % 2
    column = (c % half) // 2
    edge_low = (c == half - 1) if relayed else False
    edge_high = (c == half) if relayed else False
    before_edge = (c == half - 2) if relayed else False
    passes_on = (c < half - 2) if relayed else False
    passes_back = (c > half + 1) if relayed else False
    on_relays = [{"ctx": n} for n in range(half - 2)]
    back_relays = [{"ctx": n} for n in range(half + 2, shards)]

    def when(condition):
        return pl.when(condition) if condition is not False else (lambda f: None)

    fetches = [
        pltpu.make_async_copy(logits_in, logits, in_s.at[0]),
        pltpu.make_async_copy(docs_in, docs, in_s.at[1]),
        pltpu.make_async_copy(q_gain_in, q_gain, in_s.at[2]),
        pltpu.make_async_copy(k_gain_in, k_gain, in_s.at[3]),
        pltpu.make_async_copy(acts.at[0, 0], ownx.at[0], in_s.at[4]),
        pltpu.make_async_copy(acts.at[0, 1], ownx.at[1], in_s.at[5]),
        pltpu.make_async_copy(out_grad.at[0], dy.at[0], in_s.at[6]),
    ]
    for i in (4, 0, 1, 2, 3, 6, 5):
        fetches[i].start()

    barrier = pltpu.get_barrier_semaphore()

    def greet(other):
        pl.semaphore_signal(barrier, inc=1, device_id=other, device_id_type=MESH)

    for other in ({"ctx": prev_c}, {"ctx": next_c}, {"section": prev_s}, {"section": next_s}):
        greet(other)

    @when(edge_low)
    def _():
        for other in back_relays:
            greet(other)

    @when(edge_high)
    def _():
        for other in on_relays:
            greet(other)

    @when(passes_on)
    def _():
        greet({"ctx": half - 1})

    @when(passes_back)
    def _():
        greet({"ctx": half})

    def lanes(n):
        return pl.ds(pl.multiple_of(n * W, W), W)

    def remote(src, dst, send, recv, where):
        return pltpu.make_async_remote_copy(
            src_ref=src,
            dst_ref=dst,
            send_sem=send,
            recv_sem=recv,
            device_id=where,
            device_id_type=MESH,
        )

    t_copy = pltpu.make_async_copy(top_grad, dy.at[1], y_s)

    def each_group(f):
        def go(n, _):
            f(n)
            return 0

        lax.fori_loop(0, groups, go, 0)

    @pl.when(is_last)
    def _():
        t_copy.start()

    peers = jnp.int32(4)
    if relayed:
        peers = peers + jnp.where(edge_low, len(on_relays), 0) + jnp.where(edge_high, len(back_relays), 0)
        peers = peers + jnp.where(passes_on | passes_back, 1, 0)
    pl.semaphore_wait(barrier, peers)

    def x_copy(g, n):
        return remote(
            ownx.at[g, :, lanes(n)],
            prevx.at[g, n],
            x_s.at[g, n],
            x_r.at[g, n],
            {"ctx": next_c},
        )

    def x_far(g, n):
        return remote(
            ownx.at[g, :, lanes(n)], passing, x_s.at[g, n], f_r, {"ctx": 2 * n + g}
        )

    def x_pass():
        return remote(
            passing, prevx.at[core, column], f_s, x_r.at[core, column], {"ctx": half}
        )

    def r_copy(g, n):
        return remote(
            rsend.at[g, n], rrecv.at[g, n], r_s.at[g, n], r_r.at[g, n], {"ctx": prev_c}
        )

    def r_far(g, n):
        return remote(rsend.at[g, n], passing, r_s.at[g, n], f_r, {"ctx": half + 2 * n + g})

    def r_pass():
        return remote(
            passing, rrecv.at[core, column], f_s, r_r.at[core, column], {"ctx": half - 1}
        )

    def d_copy(n):
        return remote(
            outs.at[0, :, lanes(n)],
            dy.at[1, :, lanes(n)],
            d_s.at[n],
            d_r.at[n],
            {"section": prev_s},
        )

    def c_copy(g):
        return remote(csend.at[g], crecv.at[g], c_s.at[g], c_r.at[g], {"ctx": prev_c})

    l_copy = remote(logits.at[0], prevlog, l_s, l_r, {"ctx": next_c})

    def x_pass_in():
        x_far(0, 0).wait_recv()
        x_pass().start()

    def r_pass_in():
        r_far(0, 0).wait_recv()
        r_pass().start()

    def send_acts(g, n):
        far = edge_low & (n < groups - 1) if relayed else False

        @when(far)
        def _():
            x_far(g, n).start()

        @pl.when(has_next & jnp.logical_not(far))
        def _():
            x_copy(g, n).start()

    def send_some(g, begin, stop):
        def go(n, _):
            send_acts(g, n)
            return 0

        lax.fori_loop(begin, stop, go, 0)

    fetches[0].wait()
    fetches[4].wait()

    @pl.when(has_next)
    def _():
        l_copy.start()

    send_some(0, 0, groups // 2)

    @pl.when(jnp.logical_not(has_prev))
    def _():
        prevx[...] = jnp.zeros_like(prevx)
        prevlog[...] = jnp.zeros_like(prevlog)

    @pl.when(jnp.logical_not(has_next))
    def _():
        rrecv[...] = jnp.zeros_like(rrecv)
        crecv[...] = jnp.zeros_like(crecv)

    for i in (1, 2, 3, 6, 5):
        fetches[i].wait()

    def log_forget(x):
        return jnp.minimum(x, 0.0) - jnp.log1p(jnp.exp(-jnp.abs(x)))

    sub = lax.broadcasted_iota(jnp.int32, (rows, rows), 0)
    lane = lax.broadcasted_iota(jnp.int32, (rows, rows), 1)
    anchor = (c * rows).astype(F32)
    own_masks = []
    prev_masks = []
    n_docs = docs.shape[2]
    for g in range(2):
        d0 = lax.broadcasted_iota(jnp.int32, (n_docs, n_docs), 0)
        d1 = lax.broadcasted_iota(jnp.int32, (n_docs, n_docs), 1)
        lengths = docs[0, g : g + 1, :].astype(F32)
        bounds = jnp.sum(jnp.where(d1 <= d0, lengths, 0.0), axis=1, keepdims=True)
        pos = lax.broadcasted_iota(jnp.int32, (n_docs, rows), 1).astype(F32) + anchor
        begin = jnp.max(jnp.where(bounds <= pos, bounds, 0.0), axis=0, keepdims=True)
        key_pos = sub.astype(F32) + anchor
        own_masks.append((key_pos >= begin) & (sub <= lane))
        prev_masks.append((key_pos - float(rows) >= begin) & (sub > lane))

    @pl.when(has_prev)
    def _():
        l_copy.wait_recv()

    def make_bias(g):
        upto = (lane <= sub).astype(F32)
        after = (lane > sub).astype(F32)
        own = dot_exact(upto, log_forget(logits[0, g]), NT) * LOG2E
        before = dot_exact(after, log_forget(prevlog[g]), NT) * -LOG2E
        for h in range(heads):
            bias[g, h] = jnp.where(
                own_masks[g],
                -own[:, h : h + 1],
                jnp.where(prev_masks[g], -before[:, h : h + 1], -1e30),
            )

    make_bias(0)
    send_some(0, groups // 2, groups)

    @when(passes_on & (core == 0) if relayed else False)
    def _():
        x_pass_in()

    make_bias(1)
    factor = 1.0 / math.sqrt(D)
    upto = sub <= lane
    own_part = upto.astype(F32).astype(BF16)
    prev_part = (sub > lane).astype(F32).astype(BF16)
    own_part_t = (lane <= sub).astype(F32).astype(BF16)
    prev_part_t = (lane > sub).astype(F32).astype(BF16)

    def head(g, n, h):
        col = pl.ds(pl.multiple_of(h * D, D), D)
        here = pl.ds(pl.multiple_of((h - n * G) * D, D), D)
        x = ownx[g, :, col]
        xp = prevx[g, n, :, here]
        up = dy[g, :, col]
        gq = q_gain[:, col]
        gk = k_gain[:, col]
        xf = x.astype(F32)
        q = (xf * gq).astype(BF16)
        k = jnp.concatenate(
            [(xp.astype(F32) * gk).astype(BF16), (xf * gk).astype(BF16)], axis=0
        )
        v = jnp.concatenate([xp, x], axis=0)
        st = dot(k, q, NT)
        dpt = dot(v, up, NT)
        st = jnp.where(upto, st[rows:], st[:rows])
        dpt = jnp.where(upto, dpt[rows:], dpt[:rows])
        sc = st * (factor * LOG2E) + bias[g, h]
        e = jnp.exp2(sc - jnp.max(sc, axis=0, keepdims=True))
        p = e * (1.0 / jnp.sum(e, axis=0, keepdims=True))
        row_dot = jnp.sum(p * dpt, axis=0, keepdims=True)
        ds = (p * (dpt - row_dot)).astype(BF16)
        low = p.astype(BF16)
        sums = jnp.sum(ds.astype(F32), axis=0, keepdims=True)
        turned = ds.T
        ds_t = jnp.concatenate([turned * prev_part_t, turned * own_part_t], axis=1)
        dk = dot(jnp.concatenate([ds * prev_part, ds * own_part], axis=0), q, NN)
        dv = dot(jnp.concatenate([low * prev_part, low * own_part], axis=0), up, NN)
        dq = dot(ds_t, k, NN)
        cols = dot(jnp.ones((16, rows), BF16), ds_t, NN)[:1]
        t = (gk * factor) * dk + dv
        rsend[g, n, :, here] = t[:rows].astype(BF16)
        base[g, n, :, here] = up.astype(F32) + (gq * factor) * dq + t[rows:]
        csend[g, pl.ds(h, 1), :] = cols[:, :rows]
        diff[g, pl.ds(h, 1), :] = sums - cols[:, rows:]

    def compute(step):
        g = step // half_steps
        first = (step % half_steps) * B

        @pl.when(has_prev)
        def _():
            for b in range(B):
                x_copy(g, first + b).wait_recv()

        @pl.when((step == half_steps) & is_last)
        def _():
            t_copy.wait()

        @pl.when((g == 1) & jnp.logical_not(is_last))
        def _():
            for b in range(B):
                d_copy(first + b).wait_recv()

        def pair(i, _):
            h = first * G + 2 * i
            head(g, first, h)
            head(g, first, h + 1)
            return 0

        lax.fori_loop(0, G // 2, pair, 0)

        for b in range(B):
            n = first + b
            far = edge_high & (n > 0) if relayed else False

            @when(far)
            def _():
                r_far(g, n).start()

            @pl.when(has_prev & jnp.logical_not(far))
            def _():
                r_copy(g, n).start()

        @pl.when(has_prev & (first == groups - B))
        def _():
            c_copy(g).start()

    def finish(step):
        g = step // half_steps
        first = (step % half_steps) * B
        for b in range(B):
            n = first + b

            @pl.when(has_next)
            def _():
                r_copy(g, n).wait_recv()

            total = (base[g, n] + rrecv[g, n].astype(F32)).astype(BF16)
            outs[g, :, lanes(n)] = total

            @pl.when((g == 0) & sends_up)
            def _():
                d_copy(n).start()

            @pl.when(g == 0)
            def _():
                o_copy(0, n).start()

            @pl.when(g == 1)
            def _():
                o_copy(1, n).start()

    def o_copy(g, n):
        to = (o_first, o_second)[g]
        return pltpu.make_async_copy(outs.at[g, :, lanes(n)], to.at[0, :, lanes(n)], o_s.at[g, n])

    lag = 1

    def end(step, _):
        finish(step)
        return 0

    def one(step, _):
        compute(step)

        @pl.when((step < half_steps) & jnp.logical_not(edge_low))
        def _():
            for b in range(B):
                send_acts(1, step * B + b)

        @when(edge_low & (step == 0) if relayed else False)
        def _():
            send_some(1, 0, groups)

        @when(passes_on & (core == 1) & (step == 1) if relayed else False)
        def _():
            x_pass_in()

        @when(passes_back & (core == 0) & (step == column + 2) if relayed else False)
        def _():
            r_pass_in()

        held = (edge_low & (step <= half_steps)) | (before_edge & (step > half_steps))

        @pl.when((step >= lag) & jnp.logical_not(held))
        def _():
            finish(step - lag)

        @when(edge_low & (step == half_steps - 1) if relayed else False)
        def _():
            lax.fori_loop(0, half_steps, end, 0)

        return 0

    lax.fori_loop(0, steps, one, 0)

    @when(passes_back & (core == 1) if relayed else False)
    def _():
        r_pass_in()

    def gates(g):
        @pl.when(has_next)
        def _():
            c_copy(g).wait_recv()

        mask = own_masks[g].astype(F32)
        strict = jnp.where(sub < lane, mask, 0.0)
        forget = dot_exact(diff[g], mask, NT) + dot_exact(crecv[g], strict, NN)
        gate_out[0, g] = forget * jax.nn.sigmoid(-logits[0, g])

    gates(0)

    lax.fori_loop(jnp.where(before_edge, half_steps, steps - lag), steps, end, 0)
    gates(1)
    put_gates = pltpu.make_async_copy(gate_out, o_gate, g_s)
    put_gates.start()

    @pl.when(has_next)
    def _():
        l_copy.wait_send()

        def go(n):
            x_copy(0, n).wait_send()
            x_copy(1, n).wait_send()

        each_group(go)

    @pl.when(has_prev)
    def _():
        c_copy(0).wait_send()
        c_copy(1).wait_send()

        def go(n):
            r_copy(0, n).wait_send()
            r_copy(1, n).wait_send()

        each_group(go)

    @when(passes_on)
    def _():
        x_pass().wait_send()

    @when(passes_back)
    def _():
        r_pass().wait_send()

    @pl.when(sends_up)
    def _():
        each_group(lambda n: d_copy(n).wait_send())

    def put(n):
        o_copy(0, n).wait()
        o_copy(1, n).wait()

    each_group(put)
    put_gates.wait()


def copy_out(a, b, c, out_a, out_b, out_c, held_a, held_b, held_c, got, put):
    moves = []
    for i, (src, held, dst) in enumerate(
        ((a, held_a, out_a), (b, held_b, out_b), (c, held_c, out_c))
    ):
        moves.append(
            (
                pltpu.make_async_copy(src, held, got.at[i]),
                pltpu.make_async_copy(held, dst, put.at[i]),
            )
        )
    for into, _ in moves:
        into.start()
    for into, out in moves:
        into.wait()
        out.start()
    for _, out in moves:
        out.wait()


def body(sections, shards, acts, out_grad, top_grad, logits, q_gain, k_gain, docs):
    rows = acts.shape[2]
    heads = logits.shape[2]
    groups = heads // G
    anywhere = pl.BlockSpec(memory_space=pl.ANY)
    sem = pltpu.SemaphoreType.DMA
    vmem = pltpu.VMEM
    shapes = (
        jax.ShapeDtypeStruct(out_grad.shape, BF16),
        jax.ShapeDtypeStruct(out_grad.shape, BF16),
        jax.ShapeDtypeStruct(logits.shape, F32),
    )
    results = pl.pallas_call(
        functools.partial(kernel, sections, shards),
        out_shape=shapes,
        in_specs=[anywhere] * 7,
        out_specs=(anywhere,) * 3,
        scratch_shapes=[
            vmem(acts.shape[1:], BF16),
            vmem(logits.shape, F32),
            vmem(q_gain.shape, F32),
            vmem(k_gain.shape, F32),
            vmem(docs.shape, jnp.int32),
            vmem((2, groups, rows, W), BF16),
            vmem(acts.shape[1:], BF16),
            vmem((2, groups, rows, W), BF16),
            vmem((2, groups, rows, W), BF16),
            vmem(acts.shape[1:], BF16),
            vmem(logits.shape, F32),
            vmem((rows, W), BF16),
            vmem((2, heads, rows), F32),
            vmem((2, heads, rows), F32),
            vmem((2, heads, rows), F32),
            vmem((2, heads, rows), F32),
            vmem((2, groups, rows, W), F32),
            vmem((2, heads, rows, rows), F32),
            sem((2, groups)),
            sem((2, groups)),
            sem((2, groups)),
            sem((2, groups)),
            sem((groups,)),
            sem((groups,)),
            sem,
            sem,
            sem,
            sem,
            sem((2,)),
            sem((2,)),
            sem,
            sem((2, groups)),
            sem((7,)),
            sem,
        ],
        compiler_params=pltpu.CompilerParams(
            collective_id=0, has_side_effects=True, vmem_limit_bytes=60 * 1024 * 1024
        ),
    )(acts, out_grad, top_grad, logits, q_gain, k_gain, docs)
    return pl.pallas_call(
        copy_out,
        out_shape=shapes,
        in_specs=[anywhere] * 3,
        out_specs=(anywhere,) * 3,
        scratch_shapes=[vmem(shape.shape, shape.dtype) for shape in shapes]
        + [sem((3,)), sem((3,))],
        compiler_params=pltpu.CompilerParams(vmem_limit_bytes=60 * 1024 * 1024),
    )(*results)


def solution(mesh):
    in_specs = (
        P("section", None, "ctx", None),
        P("section", "ctx", None),
        P("ctx", None),
        P("section", None, None, "ctx"),
        P("section", None),
        P("section", None),
        P("section", None, None),
    )
    out_specs = (
        P("section", "ctx", None),
        P("section", "ctx", None),
        P("section", None, None, "ctx"),
    )
    return jax.shard_map(
        functools.partial(body, mesh.shape["section"], mesh.shape["ctx"]),
        mesh=mesh,
        in_specs=in_specs,
        out_specs=out_specs,
        check_vma=False,
    )
```
